768 devices in a mesh: dp: 64 (over z_lo, y, core), hid: 12 (over z_hi, x).
Axes of the slice: x: 4, y: 8, z: 12 (z_hi: 3, z_lo: 4; z = z_hi * 4 + z_lo), core: 2. Of those that a mesh axis runs over, the one named last changes fastest.
Arguments:
- tokens: bfloat16 [12288, 4096], P(('dp', 'hid')), may hold values from -6 to 6
- cotangent: bfloat16 [12288, 7680], P('dp', 'hid'), may hold values from -8 to 8
- weights: bfloat16 [2, 7680, 4096], P(None, 'hid'), may hold values from -0.09375 to 0.09375
- basis: bfloat16 [4096, 256], P('dp'), may hold values from -0.09375 to 0.09375
- master: float32 [2, 7680, 4096], P(None, 'hid', 'dp'), may hold values from -0.09375 to 0.09375
- first_moment: float32 [7680, 2, 256], P(('hid', 'dp')), may hold values from -48 to 48
- second_moment: float32 [7680, 2, 256], P(('hid', 'dp')), may hold values from 25 to 2500
Outputs:
- master_new: float32 [2, 7680, 4096], P(None, 'hid', 'dp')
- first_new: float32 [7680, 2, 256], P(('hid', 'dp'))
- second_new: float32 [7680, 2, 256], P(('hid', 'dp'))
The draws below stay inside these ranges and needn't reach their ends.
All inputs are finite; a program needn't handle non-finite values.
Results may differ from the reference program's by a relative error of at most 0.0003.
Values may be sent and summed in bfloat16 or wider, within the bound.
A program may use at most 64 MiB of HBM per device.

```python
import math
import jax
import jax.numpy as jnp
from jax import lax

D = 4096
FF = 7680
RANK = 256
GROUP_TOKENS = 192
TOKENS = 12288
N_DP = 64


def with_spikes(array, rng, source, target, blocks, factor):
    owner, partner = [(jnp.arange(array.shape[dim]) // (array.shape[dim] // blocks)).reshape([-1 if axis == dim else 1 for axis in range(array.ndim)]) for dim in (source, target)]
    chosen = jax.random.permutation(rng, blocks)[partner]
    strong = (owner == chosen) | (owner == (partner + blocks // 2) % blocks)
    return jnp.where(strong, factor * array, array)


def steps_of(own_key, dims, cuts, least, largest):
    loudness = 1.0
    for dim, blocks in cuts:
        steps = jax.random.uniform(jax.random.fold_in(jax.random.fold_in(own_key, 6), dim), (blocks,), jnp.float32, least / len(cuts), largest / len(cuts))
        loudness = loudness * jnp.repeat(jnp.exp(steps), dims[dim] // blocks).reshape((-1,) + (1,) * (len(dims) - 1 - dim))
    return loudness


def gaussian(key, extent, spread, limit, split=(), kind=jnp.bfloat16):
    loudness = steps_of(key, extent, split, -0.22, 0.18) if split else 1.0
    result = jax.random.normal(key, extent, jnp.float32) * spread * loudness
    return jnp.minimum(jnp.maximum(result, -limit), limit).astype(kind)


def gaussian_with(key, dims, deviation, most, pieces, heavy, held_as=jnp.bfloat16):
    entries = deviation * jax.random.normal(key, dims, jnp.float32)
    if pieces:
        entries = entries * steps_of(key, dims, pieces, -0.22, 0.18)
    return jnp.clip(with_spikes(entries, jax.random.fold_in(key, 3), *heavy), -most, most).astype(held_as)


def setup_inputs(seed: int = 0) -> dict:
    key_list = jax.random.split(jax.random.key(seed), 8)
    return {
        "tokens": gaussian(key_list[0], (TOKENS, D), 1.0, 6.0, ((0, 768),)),
        "cotangent": gaussian_with(key_list[1], (TOKENS, FF), 1.0, 8.0, ((0, 64), (1, 12)), (0, 1, 64, 4.0)),
        "weights": gaussian(key_list[2], (2, FF, D), D ** -0.5, 0.09375, ((1, 12),)),
        "basis": gaussian(key_list[3], (D, RANK), D ** -0.5, 0.09375, ((0, 64),)),
        "master": gaussian(key_list[4], (2, FF, D), D ** -0.5, 0.09375, ((1, 12), (2, 64)), jnp.float32),
        "first_moment": gaussian(key_list[5], (FF, 2, RANK), 8.0, 48.0, ((0, 768),), jnp.float32),
        "second_moment": jnp.clip(jnp.exp(math.log(2500.0) - 4.6051702 * jax.random.uniform(key_list[6], (FF, 2, RANK), jnp.float32) ** steps_of(key_list[6], (FF, 2, RANK), ((0, 768),), -0.2, 0.2)), 25.0, 2500.0),
    }


beta_first = 0.9
beta_second = 0.95
step_size = 0.05
adam_epsilon = 1e-08

def silu_pieces(pre_gate):
    sigmoid_val = jax.nn.sigmoid(pre_gate)
    return (pre_gate * sigmoid_val, sigmoid_val * (1.0 + pre_gate * (1.0 - sigmoid_val)))

def reference(tokens, cotangent, weights, basis, master, first_moment, second_moment):
    highest = lax.Precision.HIGHEST
    token_groups = tokens.reshape(N_DP, GROUP_TOKENS, D)
    cot_groups = cotangent.reshape(N_DP, GROUP_TOKENS, FF)

    def add_group(running, inputs):
        group_tokens, group_cot = inputs
        pre_gate = jnp.dot(group_tokens, weights[0].T, preferred_element_type=jnp.float32)
        pre_up = jnp.dot(group_tokens, weights[1].T, preferred_element_type=jnp.float32)
        activated, silu_slope = silu_pieces(pre_gate)
        upstream = group_cot.astype(jnp.float32)
        grad_gate = upstream * pre_up * silu_slope
        grad_up = upstream * activated
        projected = jnp.dot(group_tokens, basis, preferred_element_type=jnp.float32)
        gate_term = jnp.dot(grad_gate.T, projected, precision=highest, preferred_element_type=jnp.float32)
        up_term = jnp.dot(grad_up.T, projected, precision=highest, preferred_element_type=jnp.float32)
        return (running + jnp.stack([gate_term, up_term], axis=1), None)
    gradient, unused = lax.scan(add_group, jnp.zeros((FF, 2, RANK), jnp.float32), (token_groups, cot_groups))
    first_new = beta_first * first_moment + (1.0 - beta_first) * gradient
    second_new = beta_second * second_moment + (1.0 - beta_second) * gradient * gradient
    direction = first_new / (jnp.sqrt(second_new) + adam_epsilon)
    basis_wide = basis.astype(jnp.float32)
    gate_lift = jnp.dot(direction[:, 0, :], basis_wide.T, precision=highest, preferred_element_type=jnp.float32)
    up_lift = jnp.dot(direction[:, 1, :], basis_wide.T, precision=highest, preferred_element_type=jnp.float32)
    master_new = master - step_size * jnp.stack([gate_lift, up_lift], axis=0)
    return (master_new, first_new, second_new)
```

```python
import functools

import jax
import jax.numpy as jnp
from jax import lax
from jax.experimental import pallas as pl
from jax.experimental.pallas import tpu as pltpu
from jax.sharding import PartitionSpec as P

MESH = pl.DeviceIdType.MESH
F32 = jnp.float32
BF16 = jnp.bfloat16

beta_first = 0.9
beta_second = 0.95
step_size = 0.05
adam_epsilon = 1e-08

NX, NY, NL, NH = 4, 8, 4, 3
D, HID, RANK, TOK = 4096, 640, 256, 16
GROUP = 192
CHUNKS = 4
CW = D // CHUNKS
HALF = RANK // 2
SHARE = 10
BLOCK = 4 * SHARE
NB = NY * NL


def dot_nt(a, b):
    return lax.dot_general(a, b, (((1,), (1,)), ((), ())), preferred_element_type=F32)


def dot_nn(a, b):
    return lax.dot_general(a, b, (((1,), (0,)), ((), ())), preferred_element_type=F32)


def split(a):
    hi = a.astype(BF16)
    return hi, (a - hi.astype(F32)).astype(BF16)


def kernel(
    tok_in, cot_in, w_in, bas_in, mas_in, fm_in, sm_in,
    mas_out, fn_out, sn_out,
    tok, w, bas, cot, mas, fm, sm, fmx, smx, fmb, smb,
    cot_t, pre, grad, halves, swap, total, part_a, part_b, mid_a, mid_b, last_a, last_b,
    dirs, dirs_w, fn_b, sn_b, fn_x, sn_x,
    local_sem, z_send, z_recv, x_send, x_recv, xx_send, xx_recv,
    bz_send, bz_recv, by_send, by_recv, bf_send, bf_recv, bc_send, bc_recv,
    m_send, m_recv, s_send, s_recv, r1_send, r1_recv, r2_send, r2_recv,
    g1_send, g1_recv, g2_send, g2_recv, gc_send, gc_recv, o_send, o_recv,
):
    dp, hid = lax.axis_index("dp"), lax.axis_index("hid")
    core = lax.rem(dp, 2)
    y = lax.rem(lax.div(dp, 2), NY)
    zl = lax.div(dp, 2 * NY)
    x = lax.rem(hid, NX)
    zh = lax.div(hid, NX)

    def at(core_=core, y_=y, zl_=zl, x_=x, zh_=zh):
        return {"dp": (zl_ * NY + y_) * 2 + core_, "hid": zh_ * NX + x_}

    def turn(v, by, n):
        return lax.rem(v + (by + n), n)

    x_up, x_down = turn(x, 1, NX), turn(x, -1, NX)
    y_up, y_down = turn(y, 1, NY), turn(y, -1, NY)
    mate = at(core_=1 - core)

    peers = [at(x_=x_up), at(x_=x_down), mate]
    peers += [at(zh_=turn(zh, o, NH)) for o in range(1, NH)]
    peers += [at(zl_=turn(zl, o, NL)) for o in range(1, NL)]
    peers += [at(y_=turn(y, o, NY)) for o in range(1, NY)]

    loads = [
        pltpu.make_async_copy(tok_in, tok.at[pl.ds(pl.multiple_of(hid * TOK, TOK), TOK)], local_sem.at[0]),
        pltpu.make_async_copy(bas_in, bas.at[dp], local_sem.at[1]),
        pltpu.make_async_copy(fm_in, fm, local_sem.at[2]),
        pltpu.make_async_copy(sm_in, sm, local_sem.at[3]),
        pltpu.make_async_copy(cot_in, cot, local_sem.at[4]),
        pltpu.make_async_copy(w_in, w, local_sem.at[5]),
        pltpu.make_async_copy(mas_in, mas, local_sem.at[6]),
    ]
    for load in loads:
        load.start()

    barrier = pltpu.get_barrier_semaphore()
    for peer in peers:
        pl.semaphore_signal(barrier, inc=1, device_id=peer, device_id_type=MESH)
    pl.semaphore_wait(barrier, len(peers))

    sends = []

    def remote(src, dst, send, recv, to):
        return pltpu.make_async_remote_copy(
            src_ref=src, dst_ref=dst, send_sem=send, recv_sem=recv, device_id=to, device_id_type=MESH
        )

    def push(*args):
        copy = remote(*args)
        copy.start()
        sends.append(copy)

    def rows_of(zh_, x_):
        return pl.ds(pl.multiple_of((zh_ * NX + x_) * TOK, TOK), TOK)

    def columns(k, half=None):
        if half is None:
            return pl.ds(k * CW, CW)
        return pl.ds(k * CW + half * (CW // 2), CW // 2)

    own_rows = rows_of(zh, x)

    def z_copy(o, k, source_zh, to):
        spot = tok.at[rows_of(source_zh, x), columns(k)]
        src = tok_in.at[:, columns(k)] if o is None else spot
        return src, spot, to

    def send_z(k):
        for o in (1, 2):
            push(tok_in.at[:, columns(k)], tok.at[own_rows, columns(k)], z_send.at[o - 1, k], z_recv.at[o - 1, k],
                 at(zh_=turn(zh, o, NH)))

    def wait_z(k):
        for o in (1, 2):
            spot = tok.at[rows_of(turn(zh, -o, NH), x), columns(k)]
            remote(spot, spot, z_send.at[o - 1, k], z_recv.at[o - 1, k], at(zh_=turn(zh, -o, NH))).wait_recv()

    def send_x(h, k):
        rows = rows_of(turn(zh, -h, NH), x)
        src = tok_in.at[:, columns(k)] if h == 0 else tok.at[rows, columns(k)]
        for d, to in enumerate((x_up, x_down)):
            push(src, tok.at[rows, columns(k)], x_send.at[h, d, k], x_recv.at[h, d, k], at(x_=to))

    def pass_x(h, k):
        source = turn(zh, -h, NH)
        for d, (came, to) in enumerate(((x_down, x_up), (x_up, x_down))):
            spot = tok.at[rows_of(source, came), columns(k)]
            remote(spot, spot, x_send.at[h, d, k], x_recv.at[h, d, k], at(x_=came)).wait_recv()
            piece = tok.at[rows_of(source, came), columns(k, d)]
            push(piece, piece, xx_send.at[h, d, k], xx_recv.at[h, d, k], at(x_=to))

    def wait_xx(k):
        for h in range(NH):
            rows = rows_of(turn(zh, -h, NH), turn(x, 2, NX))
            for d in range(2):
                piece = tok.at[rows, columns(k, d)]
                remote(piece, piece, xx_send.at[h, d, k], xx_recv.at[h, d, k], at(x_=x_up)).wait_recv()

    def shard(zl_, y_, core_=core):
        return bas.at[(zl_ * NY + y_) * 2 + core_]

    def send_bz():
        for o in range(1, NL):
            push(bas_in, shard(zl, y), bz_send.at[o - 1], bz_recv.at[o - 1], at(zl_=turn(zl, o, NL)))

    def send_y(o, step):
        source = turn(zl, -o, NL)
        for d, to in enumerate((y_up, y_down)):
            sign = -1 if d == 0 else 1
            spot = shard(source, turn(y, sign * step, NY))
            if step == 3:
                spot = spot.at[pl.ds(32 * d, 32)]
                push(spot, spot, bf_send.at[o, d], bf_recv.at[o, d], at(y_=to))
            else:
                src = bas_in if o == 0 and step == 0 else spot
                push(src, spot, by_send.at[o, d, step], by_recv.at[o, d, step], at(y_=to))

    def wait_y(o, step):
        source = turn(zl, -o, NL)
        for d, came in enumerate((y_down, y_up)):
            sign = -1 if d == 0 else 1
            spot = shard(source, turn(y, sign * (step + 1), NY))
            if step == 3:
                spot = spot.at[pl.ds(32 * d, 32)]
                remote(spot, spot, bf_send.at[o, d], bf_recv.at[o, d], at(y_=came)).wait_recv()
            else:
                remote(spot, spot, by_send.at[o, d, step], by_recv.at[o, d, step], at(y_=came)).wait_recv()

    def wait_bz(o):
        spot = shard(turn(zl, -o, NL), y)
        remote(spot, spot, bz_send.at[o - 1], bz_recv.at[o - 1], at(zl_=turn(zl, -o, NL))).wait_recv()

    def send_bc(o, r):
        spot = shard(turn(zl, -o, NL), turn(y, r, NY))
        push(spot, spot, bc_send.at[o, r], bc_recv.at[o, r], mate)

    def wait_bc(o, r):
        spot = shard(turn(zl, -o, NL), turn(y, r, NY), 1 - core)
        remote(spot, spot, bc_send.at[o, r], bc_recv.at[o, r], mate).wait_recv()

    push(fm_in, fmx, m_send.at[0], m_recv.at[0], mate)
    push(sm_in, smx, m_send.at[1], m_recv.at[1], mate)
    send_bz()
    send_y(0, 0)
    for k in range(CHUNKS):
        send_z(k)
        send_x(0, k)
    loads[1].wait()
    send_bc(0, 0)

    loads[4].wait()
    cot_t[...] = cot[...].astype(F32).T

    for o in range(1, NL):
        wait_bz(o)
        send_y(o, 0)
        send_bc(o, 0)

    loads[0].wait()
    loads[5].wait()

    def products(k):
        def body(i, carry):
            rows = pl.ds(pl.multiple_of(i * HID, HID), HID)
            term = dot_nt(w[rows, columns(k)], tok[:, columns(k)])
            if k == 0:
                pre[rows, :] = term
            else:
                pre[rows, :] += term
            return carry

        lax.fori_loop(0, 2, body, 0)

    for k in range(CHUNKS):
        wait_z(k)
        send_x(1, k)
        send_x(2, k)
        pass_x(0, k)
        if k >= 1:
            pass_x(1, k - 1)
            pass_x(2, k - 1)
        for o in range(NL):
            wait_y(o, k)
            if k < 3:
                send_y(o, k + 1)
                for r in (-(k + 1), k + 1):
                    send_bc(o, r % NY)
            else:
                send_bc(o, 4)
        if k >= 2:
            wait_xx(k - 2)
            products(k - 2)
    pass_x(1, CHUNKS - 1)
    pass_x(2, CHUNKS - 1)

    loads[2].wait()
    loads[3].wait()
    for i, spot in enumerate((fmx, smx)):
        remote(spot, spot, m_send.at[i], m_recv.at[i], mate).wait_recv()
    first = core == 0
    for own, other, block in ((fm, fmx, fmb), (sm, smx, smb)):
        for g in range(2):
            mine, theirs = own[:, g, :], other[:, g, :]
            low = jnp.where(first, mine, theirs)
            high = jnp.where(first, theirs, mine)
            base = g * 2 * SHARE
            block[pl.ds(base, SHARE), :] = jnp.where(first, low[:, :HALF], low[:, HALF:])
            block[pl.ds(base + SHARE, SHARE), :] = jnp.where(first, high[:, :HALF], high[:, HALF:])

    wait_xx(CHUNKS - 2)
    products(CHUNKS - 2)
    for o in range(NL):
        for r in range(NY):
            wait_bc(o, r)
    wait_xx(CHUNKS - 1)
    products(CHUNKS - 1)

    projected = dot_nn(tok[...], bas[...].reshape(D, RANK))
    proj_hi, proj_lo = split(projected)

    def backward(i, carry):
        rows = pl.ds(pl.multiple_of(i * 320, 320), 320)
        up_rows = pl.ds(pl.multiple_of(HID + i * 320, 320), 320)
        pre_gate, pre_up, upstream = pre[rows, :], pre[up_rows, :], cot_t[rows, :]
        s = jax.nn.sigmoid(pre_gate)
        grad_gate = upstream * pre_up * (s * (1.0 + pre_gate * (1.0 - s)))
        grad_up = upstream * (pre_gate * s)
        for g, value in enumerate((grad_gate, grad_up)):
            hi, lo = split(value)
            grad[g, rows, :] = dot_nn(hi, proj_hi) + dot_nn(lo, proj_hi) + dot_nn(hi, proj_lo)
        return carry

    lax.fori_loop(0, 2, backward, 0)

    def to_blocks(m, carry):
        rows = pl.ds(pl.multiple_of(m * BLOCK, BLOCK), BLOCK)
        gate, up = grad[0, rows, :], grad[1, rows, :]
        n = 2 * SHARE
        for j in range(2):
            for h in range(2):
                lanes = slice(h * HALF, (h + 1) * HALF)
                halves[h, 2 * m + j, pl.ds(0, n), :] = gate[j * n:(j + 1) * n, lanes]
                halves[h, 2 * m + j, pl.ds(n, n), :] = up[j * n:(j + 1) * n, lanes]
        return carry

    lax.fori_loop(0, NB // 2, to_blocks, 0)

    push(halves.at[1 - core], swap, s_send, s_recv, mate)
    remote(swap, swap, s_send, s_recv, mate).wait_recv()

    def add_swap(b, carry):
        total[lax.div(b, NY), lax.rem(b, NY)] = halves[core, b] + swap[b]
        return carry

    lax.fori_loop(0, NB, add_swap, 0)

    def adam(g):
        first_new = beta_first * fmb[...] + (1.0 - beta_first) * g
        second_new = beta_second * smb[...] + (1.0 - beta_second) * g * g
        fn_b[...] = first_new
        sn_b[...] = second_new
        dirs[core, zl, y] = first_new / (jnp.sqrt(second_new) + adam_epsilon)

    def swap_outputs():
        for i, (src, dst) in enumerate(((fn_b, fn_x), (sn_b, sn_x))):
            remote(src, dst, o_send.at[i], o_recv.at[i], mate).start()

    block = dirs.at[core, zl, y]
    @pl.when(core == 0)
    def _():
        copies = []

        def go(*args):
            copy = remote(*args)
            copy.start()
            copies.append(copy)

        for o in range(1, NY):
            go(total.at[:, turn(y, o, NY)], part_a.at[o - 1], r1_send.at[o - 1], r1_recv.at[o - 1], at(y_=turn(y, o, NY)))
        value = total[:, y]
        for o in range(1, NY):
            remote(part_a.at[o - 1], part_a.at[o - 1], r1_send.at[o - 1], r1_recv.at[o - 1], at(y_=turn(y, -o, NY))).wait_recv()
            value += part_a[o - 1]
        mid_a[...] = value
        for o in range(1, NL):
            go(mid_a.at[turn(zl, o, NL)], last_a.at[o - 1], r2_send.at[o - 1], r2_recv.at[o - 1], at(zl_=turn(zl, o, NL)))
        value = mid_a[zl]
        for o in range(1, NL):
            remote(last_a.at[o - 1], last_a.at[o - 1], r2_send.at[o - 1], r2_recv.at[o - 1], at(zl_=turn(zl, -o, NL))).wait_recv()
            value += last_a[o - 1]
        adam(value)
        for o in range(1, NL):
            go(block, block, g1_send.at[o - 1], g1_recv.at[o - 1], at(zl_=turn(zl, o, NL)))
        swap_outputs()
        for o in range(1, NL):
            spot = dirs.at[core, turn(zl, -o, NL), y]
            remote(spot, spot, g1_send.at[o - 1], g1_recv.at[o - 1], at(zl_=turn(zl, -o, NL))).wait_recv()
        column = dirs.at[core, :, y]
        for o in range(1, NY):
            go(column, column, g2_send.at[o - 1], g2_recv.at[o - 1], at(y_=turn(y, o, NY)))
        go(column, column, gc_send.at[0], gc_recv.at[0], mate)
        for o in range(1, NY):
            spot = dirs.at[core, :, turn(y, -o, NY)]
            remote(spot, spot, g2_send.at[o - 1], g2_recv.at[o - 1], at(y_=turn(y, -o, NY))).wait_recv()
            go(spot, spot, gc_send.at[o], gc_recv.at[o], mate)
        for o in range(NL):
            spot = dirs.at[1 - core, turn(zl, -o, NL)]
            remote(spot, spot, gc_send.at[NY + o], gc_recv.at[NY + o], mate).wait_recv()
        for copy in copies:
            copy.wait_send()

    @pl.when(core == 1)
    def _():
        copies = []

        def go(*args):
            copy = remote(*args)
            copy.start()
            copies.append(copy)

        for o in range(1, NL):
            go(total.at[turn(zl, o, NL)], part_b.at[o - 1], r1_send.at[o - 1], r1_recv.at[o - 1], at(zl_=turn(zl, o, NL)))
        value = total[zl]
        for o in range(1, NL):
            remote(part_b.at[o - 1], part_b.at[o - 1], r1_send.at[o - 1], r1_recv.at[o - 1], at(zl_=turn(zl, -o, NL))).wait_recv()
            value += part_b[o - 1]
        mid_b[...] = value
        for o in range(1, NY):
            go(mid_b.at[turn(y, o, NY)], last_b.at[o - 1], r2_send.at[o - 1], r2_recv.at[o - 1], at(y_=turn(y, o, NY)))
        value = mid_b[y]
        for o in range(1, NY):
            remote(last_b.at[o - 1], last_b.at[o - 1], r2_send.at[o - 1], r2_recv.at[o - 1], at(y_=turn(y, -o, NY))).wait_recv()
            value += last_b[o - 1]
        adam(value)
        for o in range(1, NY):
            go(block, block, g1_send.at[o - 1], g1_recv.at[o - 1], at(y_=turn(y, o, NY)))
        swap_outputs()
        for o in range(1, NY):
            spot = dirs.at[core, zl, turn(y, -o, NY)]
            remote(spot, spot, g1_send.at[o - 1], g1_recv.at[o - 1], at(y_=turn(y, -o, NY))).wait_recv()
        row = dirs.at[core, zl]
        for o in range(1, NL):
            go(row, row, g2_send.at[o - 1], g2_recv.at[o - 1], at(zl_=turn(zl, o, NL)))
        go(row, row, gc_send.at[NY], gc_recv.at[NY], mate)
        for o in range(1, NL):
            spot = dirs.at[core, turn(zl, -o, NL)]
            remote(spot, spot, g2_send.at[o - 1], g2_recv.at[o - 1], at(zl_=turn(zl, -o, NL))).wait_recv()
            go(spot, spot, gc_send.at[NY + o], gc_recv.at[NY + o], mate)
        for o in range(NY):
            spot = dirs.at[1 - core, :, turn(y, -o, NY)]
            remote(spot, spot, gc_send.at[o], gc_recv.at[o], mate).wait_recv()
        for copy in copies:
            copy.wait_send()

    for i, (own, other, out) in enumerate(((fn_b, fn_x, fn_out), (sn_b, sn_x, sn_out))):
        copy = remote(own, other, o_send.at[i], o_recv.at[i], mate)
        copy.wait_recv()
        for g in range(2):
            base = g * 2 * SHARE
            mine = jnp.where(first, own[pl.ds(base, SHARE), :], own[pl.ds(base + SHARE, SHARE), :])
            theirs = jnp.where(first, other[pl.ds(base, SHARE), :], other[pl.ds(base + SHARE, SHARE), :])
            out[:, g, pl.ds(0, HALF)] = jnp.where(first, mine, theirs)
            out[:, g, pl.ds(HALF, HALF)] = jnp.where(first, theirs, mine)
        copy.wait_send()

    def from_blocks(m, carry):
        rows = pl.ds(pl.multiple_of(m * BLOCK, BLOCK), BLOCK)
        n = 2 * SHARE
        for h in range(2):
            lanes = pl.ds(h * HALF, HALF)
            even = dirs[h, lax.div(m, NY // 2), 2 * lax.rem(m, NY // 2)]
            odd = dirs[h, lax.div(m, NY // 2), 2 * lax.rem(m, NY // 2) + 1]
            dirs_w[0, rows, lanes] = jnp.concatenate([even[:n], odd[:n]], axis=0)
            dirs_w[1, rows, lanes] = jnp.concatenate([even[n:], odd[n:]], axis=0)
        return carry

    lax.fori_loop(0, NB // 2, from_blocks, 0)

    loads[6].wait()
    basis_own = bas[dp]
    for g in range(2):
        hi, lo = split(dirs_w[g])
        lifted = dot_nt(basis_own, hi) + dot_nt(basis_own, lo)
        mas_out[g] = mas[g] - step_size * lifted

    for copy in sends:
        copy.wait_send()


def on_device(tokens, cotangent, weights, basis, master, first_moment, second_moment):
    dma, vmem = pltpu.SemaphoreType.DMA, pltpu.VMEM
    share = (SHARE, 2, RANK)
    scratch = [
        vmem((GROUP, D), BF16), vmem((2 * HID, D), BF16), vmem((2 * NB, 64, RANK), BF16), vmem((GROUP, HID), BF16),
        vmem((2, 64, HID), F32), vmem(share, F32), vmem(share, F32), vmem(share, F32), vmem(share, F32),
        vmem((BLOCK, HALF), F32), vmem((BLOCK, HALF), F32),
        vmem((HID, GROUP), F32), vmem((2 * HID, GROUP), F32), vmem((2, HID, RANK), F32),
        vmem((2, NB, BLOCK, HALF), F32), vmem((NB, BLOCK, HALF), F32), vmem((NL, NY, BLOCK, HALF), F32),
        vmem((NY - 1, NL, BLOCK, HALF), F32), vmem((NL - 1, NY, BLOCK, HALF), F32),
        vmem((NL, BLOCK, HALF), F32), vmem((NY, BLOCK, HALF), F32),
        vmem((NL - 1, BLOCK, HALF), F32), vmem((NY - 1, BLOCK, HALF), F32),
        vmem((2, NL, NY, BLOCK, HALF), F32), vmem((2, HID, RANK), F32),
        vmem((BLOCK, HALF), F32), vmem((BLOCK, HALF), F32), vmem((BLOCK, HALF), F32), vmem((BLOCK, HALF), F32),
        dma((7,)),
    ]
    for shape in (
        (2, CHUNKS), (NH, 2, CHUNKS), (NH, 2, CHUNKS), (NL - 1,), (NL, 2, 3), (NL, 2), (NL, NY),
        (2,), None, (NY - 1,), (NY - 1,), (NY - 1,), (NY - 1,), (NY + NL,), (2,),
    ):
        scratch += [dma if shape is None else dma(shape)] * 2
    any_space = pl.BlockSpec(memory_space=pl.ANY)
    in_vmem = pl.BlockSpec(memory_space=pltpu.VMEM)
    master_new, first_new, second_new = pl.pallas_call(
        kernel,
        out_shape=(
            jax.ShapeDtypeStruct((2, 64, HID), F32),
            jax.ShapeDtypeStruct(share, F32),
            jax.ShapeDtypeStruct(share, F32),
        ),
        in_specs=[any_space] * 7,
        out_specs=(in_vmem,) * 3,
        scratch_shapes=scratch,
        compiler_params=pltpu.CompilerParams(
            collective_id=0, has_side_effects=True, vmem_limit_bytes=48 * 1024 * 1024
        ),
        name="step",
    )(
        tokens, cotangent, weights.reshape(2 * HID, D), basis, jnp.swapaxes(master, 1, 2), first_moment, second_moment
    )
    return jnp.swapaxes(master_new, 1, 2), first_new, second_new


def solution(mesh):
    in_specs = (
        P(("dp", "hid"), None),
        P("dp", "hid"),
        P(None, "hid", None),
        P("dp", None),
        P(None, "hid", "dp"),
        P(("hid", "dp"), None, None),
        P(("hid", "dp"), None, None),
    )
    out_specs = (P(None, "hid", "dp"), P(("hid", "dp"), None, None), P(("hid", "dp"), None, None))
    return jax.shard_map(
        on_device, mesh=mesh, in_specs=in_specs, out_specs=out_specs, check_vma=False
    )
```

```python
import functools

import jax
import jax.numpy as jnp
from jax import lax
from jax.experimental import pallas as pl
from jax.experimental.pallas import tpu as pltpu
from jax.sharding import PartitionSpec as P

MESH = pl.DeviceIdType.MESH
F32 = jnp.float32
BF16 = jnp.bfloat16

beta_first = 0.9
beta_second = 0.95
step_size = 0.05
adam_epsilon = 1e-08

NX, NY, NL, NH = 4, 8, 4, 3
D, HID, RANK, TOK = 4096, 640, 256, 16
GROUP = 192
CHUNKS = 4
CW = D // CHUNKS
HALF = RANK // 2
SHARE = 10
BLOCK = 4 * SHARE
NB = NY * NL


def dot_nt(a, b):
    return lax.dot_general(a, b, (((1,), (1,)), ((), ())), preferred_element_type=F32)


def dot_nn(a, b):
    return lax.dot_general(a, b, (((1,), (0,)), ((), ())), preferred_element_type=F32)


def split(a):
    hi = a.astype(BF16)
    return hi, (a - hi.astype(F32)).astype(BF16)


def kernel(
    tok_in, cot_in, w_in, bas_in, mas_in, fm_in, sm_in,
    mas_out, fn_out, sn_out,
    tok, w, bas, cot, mas, fm, sm, fmx, smx, fmb, smb,
    cot_t, pre, grad, halves, swap, total, part_a, part_b, mid_a, mid_b, last_a, last_b,
    dirs, dirs_w, fn_b, sn_b, fn_x, sn_x,
    local_sem, z_send, z_recv, x_send, x_recv, xx_send, xx_recv, xd_send, xd_recv,
    bz_send, bz_recv, ya_send, ya_recv, yb_send, yb_recv, bc_send, bc_recv,
    m_send, m_recv, s_send, s_recv, r1_send, r1_recv, r2_send, r2_recv,
    g1_send, g1_recv, ga_send, ga_recv, gb_send, gb_recv, gc_send, gc_recv, o_send, o_recv,
):
    dp, hid = lax.axis_index("dp"), lax.axis_index("hid")
    core = lax.rem(dp, 2)
    y = lax.rem(lax.div(dp, 2), NY)
    zl = lax.div(dp, 2 * NY)
    x = lax.rem(hid, NX)
    zh = lax.div(hid, NX)

    def at(core_=core, y_=y, zl_=zl, x_=x, zh_=zh):
        return {"dp": (zl_ * NY + y_) * 2 + core_, "hid": zh_ * NX + x_}

    def turn(v, by, n):
        return lax.rem(v + (by + n), n)

    x_up, x_down, x_far = turn(x, 1, NX), turn(x, -1, NX), turn(x, 2, NX)
    mate = at(core_=1 - core)

    peers = [at(x_=x_up), at(x_=x_down), at(x_=x_far), mate]
    peers += [at(zh_=turn(zh, o, NH)) for o in range(1, NH)]
    peers += [at(zl_=turn(zl, o, NL)) for o in range(1, NL)]
    peers += [at(y_=turn(y, o, NY)) for o in range(1, NY)]

    loads = [
        pltpu.make_async_copy(tok_in, tok.at[pl.ds(pl.multiple_of(hid * TOK, TOK), TOK)], local_sem.at[0]),
        pltpu.make_async_copy(bas_in, bas.at[0, y, core], local_sem.at[1]),
        pltpu.make_async_copy(fm_in, fm, local_sem.at[2]),
        pltpu.make_async_copy(sm_in, sm, local_sem.at[3]),
        pltpu.make_async_copy(cot_in, cot, local_sem.at[4]),
        pltpu.make_async_copy(w_in, w, local_sem.at[5]),
        pltpu.make_async_copy(mas_in, mas, local_sem.at[6]),
    ]
    for load in loads:
        load.start()

    barrier = pltpu.get_barrier_semaphore()
    for peer in peers:
        pl.semaphore_signal(barrier, inc=1, device_id=peer, device_id_type=MESH)
    pl.semaphore_wait(barrier, len(peers))

    sends = []

    def remote(src, dst, send, recv, to):
        return pltpu.make_async_remote_copy(
            src_ref=src, dst_ref=dst, send_sem=send, recv_sem=recv, device_id=to, device_id_type=MESH
        )

    def push(*args):
        copy = remote(*args)
        copy.start()
        sends.append(copy)

    def rows_of(zh_, x_):
        return pl.ds(pl.multiple_of((zh_ * NX + x_) * TOK, TOK), TOK)

    def columns(k, half=None):
        if half is None:
            return pl.ds(k * CW, CW)
        return pl.ds(k * CW + half * (CW // 2), CW // 2)

    own_rows = rows_of(zh, x)

    def send_z(k):
        for o in (1, 2):
            push(tok_in.at[:, columns(k)], tok.at[own_rows, columns(k)], z_send.at[o - 1, k], z_recv.at[o - 1, k],
                 at(zh_=turn(zh, o, NH)))

    def wait_z(k):
        for o in (1, 2):
            spot = tok.at[rows_of(turn(zh, -o, NH), x), columns(k)]
            remote(spot, spot, z_send.at[o - 1, k], z_recv.at[o - 1, k], at(zh_=turn(zh, -o, NH))).wait_recv()

    def send_x(h, k):
        rows = rows_of(turn(zh, -h, NH), x)
        src = tok_in.at[:, columns(k)] if h == 0 else tok.at[rows, columns(k)]
        for d, to in enumerate((x_up, x_down)):
            push(src, tok.at[rows, columns(k)], x_send.at[h, d, k], x_recv.at[h, d, k], at(x_=to))

    def pass_x(h, k):
        source = turn(zh, -h, NH)
        for d, (came, to) in enumerate(((x_down, x_up), (x_up, x_down))):
            spot = tok.at[rows_of(source, came), columns(k)]
            remote(spot, spot, x_send.at[h, d, k], x_recv.at[h, d, k], at(x_=came)).wait_recv()
            piece = tok.at[rows_of(source, came), columns(k, d)]
            push(piece, piece, xx_send.at[h, d, k], xx_recv.at[h, d, k], at(x_=to))

    def send_far(h):
        spot = tok.at[rows_of(turn(zh, -h, NH), x), columns(CHUNKS - 1)]
        push(spot, spot, xd_send.at[h - 1], xd_recv.at[h - 1], at(x_=x_far))

    def wait_x(h, k):
        for d, came in enumerate((x_down, x_up)):
            spot = tok.at[rows_of(turn(zh, -h, NH), came), columns(k)]
            remote(spot, spot, x_send.at[h, d, k], x_recv.at[h, d, k], at(x_=came)).wait_recv()

    def wait_xx(k):
        for h in range(NH):
            rows = rows_of(turn(zh, -h, NH), x_far)
            if h > 0 and k == CHUNKS - 1:
                spot = tok.at[rows, columns(k)]
                remote(spot, spot, xd_send.at[h - 1], xd_recv.at[h - 1], at(x_=x_far)).wait_recv()
                continue
            for d in range(2):
                piece = tok.at[rows, columns(k, d)]
                remote(piece, piece, xx_send.at[h, d, k], xx_recv.at[h, d, k], at(x_=x_up)).wait_recv()

    def shards(part, by, half=None, core_=core):
        spot = (0 if part == 0 else pl.ds(1, NL - 1), turn(y, by, NY), core_)
        return bas.at[spot if half is None else spot + (pl.ds(32 * half, 32),)]

    steps = (1, -1, 2, -2)
    later = ((-3, None), (-4, 0), (3, None), (4, 1))

    def send_bz():
        for o in range(1, NL):
            push(bas_in, bas.at[o, y, core], bz_send.at[o - 1], bz_recv.at[o - 1], at(zl_=turn(zl, o, NL)))

    def wait_bz():
        for o in range(1, NL):
            spot = bas.at[o, y, core]
            remote(spot, spot, bz_send.at[o - 1], bz_recv.at[o - 1], at(zl_=turn(zl, -o, NL))).wait_recv()

    def send_ya(part):
        for i, step in enumerate(steps):
            src = bas_in if part == 0 else shards(1, 0)
            push(src, shards(part, 0), ya_send.at[part, i], ya_recv.at[part, i], at(y_=turn(y, step, NY)))

    def pass_y(part):
        for i in (2, 3, 0, 1):
            spot = shards(part, -steps[i])
            remote(spot, spot, ya_send.at[part, i], ya_recv.at[part, i], at(y_=turn(y, -steps[i], NY))).wait_recv()
            if i >= 2:
                sign, d = (1, 0) if i == 2 else (-1, 1)
                push(spot, spot, yb_send.at[part, 2 * d], yb_recv.at[part, 2 * d], at(y_=turn(y, sign, NY)))
                piece = shards(part, -steps[i], d)
                push(piece, piece, yb_send.at[part, 2 * d + 1], yb_recv.at[part, 2 * d + 1], at(y_=turn(y, 2 * sign, NY)))

    def wait_yb(part):
        for i, (by, half) in enumerate(later):
            spot = shards(part, by, half)
            remote(spot, spot, yb_send.at[part, i], yb_recv.at[part, i], at(y_=turn(y, 1, NY))).wait_recv()

    def send_bc(by):
        spot = bas.at[:, turn(y, by, NY), core]
        push(spot, spot, bc_send.at[by % NY], bc_recv.at[by % NY], mate)

    def wait_bc():
        for by in range(NY):
            spot = bas.at[:, turn(y, by, NY), 1 - core]
            remote(spot, spot, bc_send.at[by], bc_recv.at[by], mate).wait_recv()

    def products(k):
        def body(i, carry):
            rows = pl.ds(pl.multiple_of(i * HID, HID), HID)
            term = dot_nt(w[rows, columns(k)], tok[:, columns(k)])
            if k == 0:
                pre[rows, :] = term
            else:
                pre[rows, :] += term
            return carry

        lax.fori_loop(0, 2, body, 0)

    send_bz()
    send_z(0)
    send_ya(0)
    for k in range(CHUNKS):
        send_x(0, k)
    send_z(1)
    push(fm_in, fmx, m_send.at[0], m_recv.at[0], mate)
    push(sm_in, smx, m_send.at[1], m_recv.at[1], mate)
    loads[1].wait()
    loads[4].wait()
    wait_bz()
    send_ya(1)
    send_bc(0)
    cot_t[...] = cot[...].astype(F32).T

    wait_z(0)
    send_z(2)
    send_x(1, 0)
    send_x(2, 0)
    pass_x(0, 0)
    pass_x(0, 1)
    pass_y(0)
    wait_z(1)
    send_z(3)
    send_x(1, 1)
    send_x(2, 1)
    pass_x(0, 2)
    pass_x(0, 3)
    pass_x(1, 0)
    pass_x(2, 0)
    wait_z(2)
    send_x(1, 2)
    send_x(2, 2)
    pass_y(1)
    for by in (1, -1, 2, -2):
        send_bc(by)
    pass_x(1, 1)
    pass_x(2, 1)
    wait_z(3)
    send_x(1, 3)
    send_x(2, 3)
    send_far(1)
    send_far(2)
    pass_x(1, 2)
    pass_x(2, 2)
    loads[0].wait()
    loads[5].wait()
    wait_xx(0)
    products(0)
    wait_yb(0)
    wait_yb(1)
    for by in (3, -3, 4):
        send_bc(by)
    wait_xx(1)
    products(1)

    loads[2].wait()
    loads[3].wait()
    for i, spot in enumerate((fmx, smx)):
        remote(spot, spot, m_send.at[i], m_recv.at[i], mate).wait_recv()
    first = core == 0
    for own, other, block in ((fm, fmx, fmb), (sm, smx, smb)):
        for g in range(2):
            mine, theirs = own[:, g, :], other[:, g, :]
            low = jnp.where(first, mine, theirs)
            high = jnp.where(first, theirs, mine)
            base = g * 2 * SHARE
            block[pl.ds(base, SHARE), :] = jnp.where(first, low[:, :HALF], low[:, HALF:])
            block[pl.ds(base + SHARE, SHARE), :] = jnp.where(first, high[:, :HALF], high[:, HALF:])

    wait_xx(2)
    products(2)
    wait_bc()
    wait_x(1, 3)
    wait_x(2, 3)
    wait_xx(3)
    products(3)

    projected = None
    for o in range(NL):
        slab = pl.ds(pl.multiple_of(turn(zl, -o, NL) * (D // NL), D // NL), D // NL)
        term = dot_nn(tok[:, slab], bas[o].reshape(D // NL, RANK))
        projected = term if o == 0 else projected + term
    proj_hi, proj_lo = split(projected)

    PART = HID // 2

    def to_blocks(m, carry):
        rows = pl.ds(pl.multiple_of(m * BLOCK, BLOCK), BLOCK)
        gate, up = grad[0, rows, :], grad[1, rows, :]
        n = 2 * SHARE
        for j in range(2):
            for h in range(2):
                lanes = slice(h * HALF, (h + 1) * HALF)
                halves[h, 2 * m + j, pl.ds(0, n), :] = gate[j * n:(j + 1) * n, lanes]
                halves[h, 2 * m + j, pl.ds(n, n), :] = up[j * n:(j + 1) * n, lanes]
        return carry

    def swap_part(i):
        part = pl.ds(i * (NB // 2), NB // 2)
        return halves.at[1 - core, part], swap.at[part], s_send.at[i], s_recv.at[i], mate

    for i in range(2):
        rows, up_rows = pl.ds(i * PART, PART), pl.ds(HID + i * PART, PART)
        pre_gate, pre_up, upstream = pre[rows, :], pre[up_rows, :], cot_t[rows, :]
        s = jax.nn.sigmoid(pre_gate)
        grad_gate = upstream * pre_up * (s * (1.0 + pre_gate * (1.0 - s)))
        grad_up = upstream * (pre_gate * s)
        for g, value in enumerate((grad_gate, grad_up)):
            hi, lo = split(value)
            grad[g, rows, :] = dot_nn(hi, proj_hi) + dot_nn(lo, proj_hi) + dot_nn(hi, proj_lo)
        lax.fori_loop(i * (NB // 4), (i + 1) * (NB // 4), to_blocks, 0)
        push(*swap_part(i))

    def add_part(i):
        remote(*swap_part(i)).wait_recv()

        def add_swap(b, carry):
            total[lax.div(b, NY), lax.rem(b, NY)] = halves[core, b] + swap[b]
            return carry

        lax.fori_loop(i * (NB // 2), (i + 1) * (NB // 2), add_swap, 0)

    def adam(g):
        first_new = beta_first * fmb[...] + (1.0 - beta_first) * g
        second_new = beta_second * smb[...] + (1.0 - beta_second) * g * g
        fn_b[...] = first_new
        sn_b[...] = second_new
        return first_new / (jnp.sqrt(second_new) + adam_epsilon)

    def swap_outputs():
        for i, (src, dst) in enumerate(((fn_b, fn_x), (sn_b, sn_x))):
            remote(src, dst, o_send.at[i], o_recv.at[i], mate).start()

    @pl.when(core == 0)
    def _():
        copies = []

        def go(*args):
            copy = remote(*args)
            copy.start()
            copies.append(copy)

        def came(spot, send, recv):
            remote(spot, spot, send, recv, mate).wait_recv()

        for i in range(2):
            add_part(i)
            part = pl.ds(i * (NL // 2), NL // 2)
            for o in range(1, NY):
                go(total.at[part, turn(y, o, NY)], part_a.at[o - 1, part], r1_send.at[i, o - 1], r1_recv.at[i, o - 1],
                   at(y_=turn(y, o, NY)))
        for i in range(2):
            part = pl.ds(i * (NL // 2), NL // 2)
            value = total[part, y]
            for o in range(1, NY):
                came(part_a.at[o - 1, part], r1_send.at[i, o - 1], r1_recv.at[i, o - 1])
                value += part_a[o - 1, part]
            mid_a[part] = value
        for o in range(1, NL):
            go(mid_a.at[turn(zl, o, NL)], last_a.at[o - 1], r2_send.at[o - 1], r2_recv.at[o - 1], at(zl_=turn(zl, o, NL)))
        value = mid_a[zl]
        for o in range(1, NL):
            came(last_a.at[o - 1], r2_send.at[o - 1], r2_recv.at[o - 1])
            value += last_a[o - 1]
        own, rest = dirs.at[0, 0, y], dirs.at[0, pl.ds(1, NL - 1), y]
        dirs[0, 0, y] = adam(value)
        for o in range(1, NL):
            go(own, dirs.at[0, o, y], g1_send.at[o - 1], g1_recv.at[o - 1], at(zl_=turn(zl, o, NL)))
        for o in range(1, NY):
            go(own, own, ga_send.at[o - 1], ga_recv.at[o - 1], at(y_=turn(y, o, NY)))
        swap_outputs()
        for o in range(1, NL):
            came(dirs.at[0, o, y], g1_send.at[o - 1], g1_recv.at[o - 1])
        for o in range(1, NY):
            go(rest, rest, gb_send.at[o - 1], gb_recv.at[o - 1], at(y_=turn(y, o, NY)))
        go(dirs.at[0, :, y], dirs.at[0, :, y], gc_send.at[0], gc_recv.at[0], mate)
        for o in range(1, NY):
            source = turn(y, -o, NY)
            came(dirs.at[0, 0, source], ga_send.at[o - 1], ga_recv.at[o - 1])
            came(dirs.at[0, pl.ds(1, NL - 1), source], gb_send.at[o - 1], gb_recv.at[o - 1])
            go(dirs.at[0, :, source], dirs.at[0, :, source], gc_send.at[o], gc_recv.at[o], mate)
        for o in range(NL):
            came(dirs.at[1, turn(zl, -o, NL)], gc_send.at[NY + o], gc_recv.at[NY + o])
        for copy in copies:
            copy.wait_send()

    @pl.when(core == 1)
    def _():
        copies = []

        def go(*args):
            copy = remote(*args)
            copy.start()
            copies.append(copy)

        def came(spot, send, recv):
            remote(spot, spot, send, recv, mate).wait_recv()

        firsts = []
        for o in range(1, NL):
            to = turn(zl, o, NL)
            firsts.append((to, remote(total.at[to], part_b.at[o - 1], r1_send.at[0, o - 1], r1_recv.at[0, o - 1], at(zl_=to))))
        for i in range(2):
            add_part(i)
            for to, copy in firsts:
                pl.when(lax.div(to, NL // 2) == i)(copy.start)
        value = total[zl]
        for o in range(1, NL):
            came(part_b.at[o - 1], r1_send.at[0, o - 1], r1_recv.at[0, o - 1])
            value += part_b[o - 1]
        mid_b[...] = value
        for o in range(1, NY):
            go(mid_b.at[turn(y, o, NY)], last_b.at[o - 1], r2_send.at[o - 1], r2_recv.at[o - 1], at(y_=turn(y, o, NY)))
        value = mid_b[y]
        for o in range(1, NY):
            came(last_b.at[o - 1], r2_send.at[o - 1], r2_recv.at[o - 1])
            value += last_b[o - 1]
        own, rest = dirs.at[1, zl, 0], dirs.at[1, zl, pl.ds(1, NY - 1)]
        dirs[1, zl, 0] = adam(value)
        for o in range(1, NY):
            go(own, dirs.at[1, zl, o], g1_send.at[o - 1], g1_recv.at[o - 1], at(y_=turn(y, o, NY)))
        for o in range(1, NL):
            go(own, own, ga_send.at[o - 1], ga_recv.at[o - 1], at(zl_=turn(zl, o, NL)))
        swap_outputs()
        for o in range(1, NY):
            came(dirs.at[1, zl, o], g1_send.at[o - 1], g1_recv.at[o - 1])
        for o in range(1, NL):
            go(rest, rest, gb_send.at[o - 1], gb_recv.at[o - 1], at(zl_=turn(zl, o, NL)))
        go(dirs.at[1, zl], dirs.at[1, zl], gc_send.at[NY], gc_recv.at[NY], mate)
        for o in range(1, NL):
            source = turn(zl, -o, NL)
            came(dirs.at[1, source, 0], ga_send.at[o - 1], ga_recv.at[o - 1])
            came(dirs.at[1, source, pl.ds(1, NY - 1)], gb_send.at[o - 1], gb_recv.at[o - 1])
            go(dirs.at[1, source], dirs.at[1, source], gc_send.at[NY + o], gc_recv.at[NY + o], mate)
        for o in range(NY):
            source = turn(y, -o, NY)
            came(dirs.at[0, :, source], gc_send.at[o], gc_recv.at[o])
        for to, copy in firsts:
            copy.wait_send()
        for copy in copies:
            copy.wait_send()

    for i, (own, other, out) in enumerate(((fn_b, fn_x, fn_out), (sn_b, sn_x, sn_out))):
        copy = remote(own, other, o_send.at[i], o_recv.at[i], mate)
        copy.wait_recv()
        for g in range(2):
            base = g * 2 * SHARE
            mine = jnp.where(first, own[pl.ds(base, SHARE), :], own[pl.ds(base + SHARE, SHARE), :])
            theirs = jnp.where(first, other[pl.ds(base, SHARE), :], other[pl.ds(base + SHARE, SHARE), :])
            out[:, g, pl.ds(0, HALF)] = jnp.where(first, mine, theirs)
            out[:, g, pl.ds(HALF, HALF)] = jnp.where(first, theirs, mine)
        copy.wait_send()

    def from_blocks(m, carry):
        rows = pl.ds(pl.multiple_of(m * BLOCK, BLOCK), BLOCK)
        n = 2 * SHARE
        for h in range(2):
            lanes = pl.ds(h * HALF, HALF)
            z_, y_ = lax.div(m, NY // 2), 2 * lax.rem(m, NY // 2)
            if h == 0:
                back = lax.rem(zl - z_ + NL, NL)
                even, odd = dirs[0, back, y_], dirs[0, back, y_ + 1]
            else:
                even = dirs[1, z_, lax.rem(y - y_ + NY, NY)]
                odd = dirs[1, z_, lax.rem(y - y_ - 1 + NY, NY)]
            dirs_w[0, rows, lanes] = jnp.concatenate([even[:n], odd[:n]], axis=0)
            dirs_w[1, rows, lanes] = jnp.concatenate([even[n:], odd[n:]], axis=0)
        return carry

    lax.fori_loop(0, NB // 2, from_blocks, 0)

    loads[6].wait()
    basis_own = bas[0, y, core]
    for g in range(2):
        hi, lo = split(dirs_w[g])
        lifted = dot_nt(basis_own, hi) + dot_nt(basis_own, lo)
        mas_out[g] = mas[g] - step_size * lifted

    for copy in sends:
        copy.wait_send()


def on_device(tokens, cotangent, weights, basis, master, first_moment, second_moment):
    dma, vmem = pltpu.SemaphoreType.DMA, pltpu.VMEM
    share = (SHARE, 2, RANK)
    scratch = [
        vmem((GROUP, D), BF16), vmem((2 * HID, D), BF16), vmem((NL, NY, 2, 64, RANK), BF16), vmem((GROUP, HID), BF16),
        vmem((2, 64, HID), F32), vmem(share, F32), vmem(share, F32), vmem(share, F32), vmem(share, F32),
        vmem((BLOCK, HALF), F32), vmem((BLOCK, HALF), F32),
        vmem((HID, GROUP), F32), vmem((2 * HID, GROUP), F32), vmem((2, HID, RANK), F32),
        vmem((2, NB, BLOCK, HALF), F32), vmem((NB, BLOCK, HALF), F32), vmem((NL, NY, BLOCK, HALF), F32),
        vmem((NY - 1, NL, BLOCK, HALF), F32), vmem((NL - 1, NY, BLOCK, HALF), F32),
        vmem((NL, BLOCK, HALF), F32), vmem((NY, BLOCK, HALF), F32),
        vmem((NL - 1, BLOCK, HALF), F32), vmem((NY - 1, BLOCK, HALF), F32),
        vmem((2, NL, NY, BLOCK, HALF), F32), vmem((2, HID, RANK), F32),
        vmem((BLOCK, HALF), F32), vmem((BLOCK, HALF), F32), vmem((BLOCK, HALF), F32), vmem((BLOCK, HALF), F32),
        dma((7,)),
    ]
    for shape in (
        (2, CHUNKS), (NH, 2, CHUNKS), (NH, 2, CHUNKS), (2,), (NL - 1,), (2, 4), (2, 4), (NY,),
        (2,), (2,), (2, NY - 1), (NY - 1,), (NY - 1,), (NY - 1,), (NY - 1,), (NY + NL,), (2,),
    ):
        scratch += [dma if shape is None else dma(shape)] * 2
    any_space = pl.BlockSpec(memory_space=pl.ANY)
    in_vmem = pl.BlockSpec(memory_space=pltpu.VMEM)
    master_new, first_new, second_new = pl.pallas_call(
        kernel,
        out_shape=(
            jax.ShapeDtypeStruct((2, 64, HID), F32),
            jax.ShapeDtypeStruct(share, F32),
            jax.ShapeDtypeStruct(share, F32),
        ),
        in_specs=[any_space] * 7,
        out_specs=(in_vmem,) * 3,
        scratch_shapes=scratch,
        compiler_params=pltpu.CompilerParams(
            collective_id=0, has_side_effects=True, vmem_limit_bytes=63 * 1024 * 1024
        ),
        name="step",
    )(
        tokens, cotangent, weights.reshape(2 * HID, D), basis, jnp.swapaxes(master, 1, 2), first_moment, second_moment
    )
    return jnp.swapaxes(master_new, 1, 2), first_new, second_new


def solution(mesh):
    in_specs = (
        P(("dp", "hid"), None),
        P("dp", "hid"),
        P(None, "hid", None),
        P("dp", None),
        P(None, "hid", "dp"),
        P(("hid", "dp"), None, None),
        P(("hid", "dp"), None, None),
    )
    out_specs = (P(None, "hid", "dp"), P(("hid", "dp"), None, None), P(("hid", "dp"), None, None))
    return jax.shard_map(
        on_device, mesh=mesh, in_specs=in_specs, out_specs=out_specs, check_vma=False
    )
```

```python
import functools

import jax
import jax.numpy as jnp
from jax import lax
from jax.experimental import pallas as pl
from jax.experimental.pallas import tpu as pltpu
from jax.sharding import PartitionSpec as P

MESH = pl.DeviceIdType.MESH
F32 = jnp.float32
BF16 = jnp.bfloat16

beta_first = 0.9
beta_second = 0.95
step_size = 0.05
adam_epsilon = 1e-08

NX, NY, NL, NH = 4, 8, 4, 3
D, HID, RANK, TOK = 4096, 640, 256, 16
GROUP = 192
CHUNKS = 4
CW = D // CHUNKS
HALF = RANK // 2
SHARE = 10
BLOCK = 4 * SHARE
NB = NY * NL
CUT = 24


def dot_nt(a, b):
    return lax.dot_general(a, b, (((1,), (1,)), ((), ())), preferred_element_type=F32)


def dot_nn(a, b):
    return lax.dot_general(a, b, (((1,), (0,)), ((), ())), preferred_element_type=F32)


def split(a):
    hi = a.astype(BF16)
    return hi, (a - hi.astype(F32)).astype(BF16)


def kernel(
    tok_in, cot_in, w_in, bas_in, mas_in, fm_in, sm_in,
    mas_out, fn_out, sn_out,
    tok, w, bas, cot, mas, fm, sm, fmx, smx, fmb, smb,
    cot_t, pre, grad, halves, swap, total_y, total_z, part_y, part_z, mid_y, mid_z, last_y, last_z,
    dirs_y, dirs_z, dirs_w, fn_b, sn_b, fn_x, sn_x,
    local_sem, z_send, z_recv, x_send, x_recv, xx_send, xx_recv, xd_send, xd_recv,
    bz_send, bz_recv, ya_send, ya_recv, yb_send, yb_recv, bc_send, bc_recv,
    m_send, m_recv, s_send, s_recv, ry_send, ry_recv, rz_send, rz_recv, ty_send, ty_recv, tz_send, tz_recv,
    gz_send, gz_recv, gy_send, gy_recv, ga_send, ga_recv, gb_send, gb_recv, gc_send, gc_recv, gd_send, gd_recv,
    gm_send, gm_recv, o_send, o_recv,
):
    dp, hid = lax.axis_index("dp"), lax.axis_index("hid")
    core = lax.rem(dp, 2)
    y = lax.rem(lax.div(dp, 2), NY)
    zl = lax.div(dp, 2 * NY)
    x = lax.rem(hid, NX)
    zh = lax.div(hid, NX)

    def at(core_=core, y_=y, zl_=zl, x_=x, zh_=zh):
        return {"dp": (zl_ * NY + y_) * 2 + core_, "hid": zh_ * NX + x_}

    def turn(v, by, n):
        return lax.rem(v + (by + n), n)

    x_up, x_down, x_far = turn(x, 1, NX), turn(x, -1, NX), turn(x, 2, NX)
    mate = at(core_=1 - core)

    peers = [at(x_=x_up), at(x_=x_down), at(x_=x_far), mate]
    peers += [at(zh_=turn(zh, o, NH)) for o in range(1, NH)]
    peers += [at(zl_=turn(zl, o, NL)) for o in range(1, NL)]
    peers += [at(y_=turn(y, o, NY)) for o in range(1, NY)]

    loads = [
        pltpu.make_async_copy(tok_in, tok.at[pl.ds(pl.multiple_of(hid * TOK, TOK), TOK)], local_sem.at[0]),
        pltpu.make_async_copy(bas_in, bas.at[0, y, core], local_sem.at[1]),
        pltpu.make_async_copy(fm_in, fm, local_sem.at[2]),
        pltpu.make_async_copy(sm_in, sm, local_sem.at[3]),
        pltpu.make_async_copy(cot_in, cot, local_sem.at[4]),
        pltpu.make_async_copy(w_in, w, local_sem.at[5]),
        pltpu.make_async_copy(mas_in, mas, local_sem.at[6]),
    ]
    for load in loads:
        load.start()

    barrier = pltpu.get_barrier_semaphore()
    for peer in peers:
        pl.semaphore_signal(barrier, inc=1, device_id=peer, device_id_type=MESH)
    pl.semaphore_wait(barrier, len(peers))

    sends = []

    def remote(src, dst, send, recv, to):
        return pltpu.make_async_remote_copy(
            src_ref=src, dst_ref=dst, send_sem=send, recv_sem=recv, device_id=to, device_id_type=MESH
        )

    def push(*args):
        copy = remote(*args)
        copy.start()
        sends.append(copy)

    def rows_of(zh_, x_):
        return pl.ds(pl.multiple_of((zh_ * NX + x_) * TOK, TOK), TOK)

    def columns(k, half=None):
        if half is None:
            return pl.ds(k * CW, CW)
        return pl.ds(k * CW + half * (CW // 2), CW // 2)

    own_rows = rows_of(zh, x)

    def send_z(k):
        for o in (1, 2):
            push(tok_in.at[:, columns(k)], tok.at[own_rows, columns(k)], z_send.at[o - 1, k], z_recv.at[o - 1, k],
                 at(zh_=turn(zh, o, NH)))

    def wait_z(k):
        for o in (1, 2):
            spot = tok.at[rows_of(turn(zh, -o, NH), x), columns(k)]
            remote(spot, spot, z_send.at[o - 1, k], z_recv.at[o - 1, k], at(zh_=turn(zh, -o, NH))).wait_recv()

    def send_x(h, k):
        rows = rows_of(turn(zh, -h, NH), x)
        src = tok_in.at[:, columns(k)] if h == 0 else tok.at[rows, columns(k)]
        for d, to in enumerate((x_up, x_down)):
            push(src, tok.at[rows, columns(k)], x_send.at[h, d, k], x_recv.at[h, d, k], at(x_=to))

    def pass_x(h, k):
        source = turn(zh, -h, NH)
        for d, (came, to) in enumerate(((x_down, x_up), (x_up, x_down))):
            spot = tok.at[rows_of(source, came), columns(k)]
            remote(spot, spot, x_send.at[h, d, k], x_recv.at[h, d, k], at(x_=came)).wait_recv()
            piece = tok.at[rows_of(source, came), columns(k, d)]
            push(piece, piece, xx_send.at[h, d, k], xx_recv.at[h, d, k], at(x_=to))

    def send_far(h):
        spot = tok.at[rows_of(turn(zh, -h, NH), x), columns(CHUNKS - 1)]
        push(spot, spot, xd_send.at[h - 1], xd_recv.at[h - 1], at(x_=x_far))

    def wait_x(h, k):
        for d, came in enumerate((x_down, x_up)):
            spot = tok.at[rows_of(turn(zh, -h, NH), came), columns(k)]
            remote(spot, spot, x_send.at[h, d, k], x_recv.at[h, d, k], at(x_=came)).wait_recv()

    def wait_xx(k):
        for h in range(NH):
            rows = rows_of(turn(zh, -h, NH), x_far)
            if h > 0 and k == CHUNKS - 1:
                spot = tok.at[rows, columns(k)]
                remote(spot, spot, xd_send.at[h - 1], xd_recv.at[h - 1], at(x_=x_far)).wait_recv()
                continue
            for d in range(2):
                piece = tok.at[rows, columns(k, d)]
                remote(piece, piece, xx_send.at[h, d, k], xx_recv.at[h, d, k], at(x_=x_up)).wait_recv()

    def shards(part, by, half=None, core_=core):
        spot = (0 if part == 0 else pl.ds(1, NL - 1), turn(y, by, NY), core_)
        return bas.at[spot if half is None else spot + (pl.ds(32 * half, 32),)]

    steps = (1, -1, 2, -2)
    later = ((-3, None), (-4, 0), (3, None), (4, 1))

    def send_bz():
        for o in range(1, NL):
            push(bas_in, bas.at[o, y, core], bz_send.at[o - 1], bz_recv.at[o - 1], at(zl_=turn(zl, o, NL)))

    def wait_bz():
        for o in range(1, NL):
            spot = bas.at[o, y, core]
            remote(spot, spot, bz_send.at[o - 1], bz_recv.at[o - 1], at(zl_=turn(zl, -o, NL))).wait_recv()

    def send_ya(part):
        for i, step in enumerate(steps):
            src = bas_in if part == 0 else shards(1, 0)
            push(src, shards(part, 0), ya_send.at[part, i], ya_recv.at[part, i], at(y_=turn(y, step, NY)))

    def pass_y(part):
        for i in (2, 3, 0, 1):
            spot = shards(part, -steps[i])
            remote(spot, spot, ya_send.at[part, i], ya_recv.at[part, i], at(y_=turn(y, -steps[i], NY))).wait_recv()
            if i >= 2:
                sign, d = (1, 0) if i == 2 else (-1, 1)
                push(spot, spot, yb_send.at[part, 2 * d], yb_recv.at[part, 2 * d], at(y_=turn(y, sign, NY)))
                piece = shards(part, -steps[i], d)
                push(piece, piece, yb_send.at[part, 2 * d + 1], yb_recv.at[part, 2 * d + 1], at(y_=turn(y, 2 * sign, NY)))

    def wait_yb(part):
        for i, (by, half) in enumerate(later):
            spot = shards(part, by, half)
            remote(spot, spot, yb_send.at[part, i], yb_recv.at[part, i], at(y_=turn(y, 1, NY))).wait_recv()

    def send_bc(by):
        spot = bas.at[:, turn(y, by, NY), core]
        push(spot, spot, bc_send.at[by % NY], bc_recv.at[by % NY], mate)

    def wait_bc():
        for by in range(NY):
            spot = bas.at[:, turn(y, by, NY), 1 - core]
            remote(spot, spot, bc_send.at[by], bc_recv.at[by], mate).wait_recv()

    def products(k):
        def body(i, carry):
            rows = pl.ds(pl.multiple_of(i * HID, HID), HID)
            term = dot_nt(w[rows, columns(k)], tok[:, columns(k)])
            if k == 0:
                pre[rows, :] = term
            else:
                pre[rows, :] += term
            return carry

        lax.fori_loop(0, 2, body, 0)

    def project(k):
        slab = bas[turn(zl, -k, NL)].reshape(CW, RANK)
        return dot_nn(tok[:, columns(k)], slab)

    send_bz()
    send_z(0)
    send_ya(0)
    for k in range(CHUNKS):
        send_x(0, k)
    send_z(1)
    push(fm_in, fmx, m_send.at[0], m_recv.at[0], mate)
    push(sm_in, smx, m_send.at[1], m_recv.at[1], mate)
    loads[1].wait()
    loads[4].wait()
    wait_bz()
    send_ya(1)
    send_bc(0)
    cot_t[...] = cot[...].astype(F32).T

    wait_z(0)
    send_z(2)
    send_x(1, 0)
    send_x(2, 0)
    pass_x(0, 0)
    pass_x(0, 1)
    pass_y(0)
    wait_z(1)
    send_z(3)
    send_x(1, 1)
    send_x(2, 1)
    pass_x(0, 2)
    pass_x(0, 3)
    pass_x(1, 0)
    pass_x(2, 0)
    wait_z(2)
    send_x(1, 2)
    send_x(2, 2)
    pass_y(1)
    for by in (1, -1, 2, -2):
        send_bc(by)
    pass_x(1, 1)
    pass_x(2, 1)
    wait_z(3)
    send_x(1, 3)
    send_x(2, 3)
    send_far(1)
    send_far(2)
    pass_x(1, 2)
    pass_x(2, 2)
    loads[0].wait()
    loads[5].wait()
    wait_xx(0)
    products(0)
    wait_yb(0)
    wait_yb(1)
    for by in (3, -3, 4):
        send_bc(by)
    wait_xx(1)
    products(1)

    loads[2].wait()
    loads[3].wait()
    for i, spot in enumerate((fmx, smx)):
        remote(spot, spot, m_send.at[i], m_recv.at[i], mate).wait_recv()
    first = core == 0
    for own, other, block in ((fm, fmx, fmb), (sm, smx, smb)):
        for g in range(2):
            mine, theirs = own[:, g, :], other[:, g, :]
            low = jnp.where(first, mine, theirs)
            high = jnp.where(first, theirs, mine)
            base = g * 2 * SHARE
            block[pl.ds(base, SHARE), :] = jnp.where(first, low[:, :HALF], low[:, HALF:])
            block[pl.ds(base + SHARE, SHARE), :] = jnp.where(first, high[:, :HALF], high[:, HALF:])

    wait_xx(2)
    products(2)
    wait_bc()
    projected = project(0)
    for k in range(1, CHUNKS - 1):
        projected += project(k)
    wait_x(1, 3)
    wait_x(2, 3)
    wait_xx(3)
    products(3)

    proj_hi, proj_lo = split(projected + project(CHUNKS - 1))

    PART = HID // 2

    def to_blocks(m, carry):
        rows = pl.ds(pl.multiple_of(m * BLOCK, BLOCK), BLOCK)
        gate, up = grad[0, rows, :], grad[1, rows, :]
        n = 2 * SHARE
        for j in range(2):
            for h in range(2):
                lanes = slice(h * HALF, (h + 1) * HALF)
                halves[h, 2 * m + j, pl.ds(0, n), :] = gate[j * n:(j + 1) * n, lanes]
                halves[h, 2 * m + j, pl.ds(n, n), :] = up[j * n:(j + 1) * n, lanes]
        return carry

    def swap_part(i):
        part = pl.ds(i * (NB // 2), NB // 2)
        return halves.at[1 - core, part], swap.at[part], s_send.at[i], s_recv.at[i], mate

    for i in range(2):
        rows, up_rows = pl.ds(i * PART, PART), pl.ds(HID + i * PART, PART)
        pre_gate, pre_up, upstream = pre[rows, :], pre[up_rows, :], cot_t[rows, :]
        s = jax.nn.sigmoid(pre_gate)
        grad_gate = upstream * pre_up * (s * (1.0 + pre_gate * (1.0 - s)))
        grad_up = upstream * (pre_gate * s)
        for g, value in enumerate((grad_gate, grad_up)):
            hi, lo = split(value)
            grad[g, rows, :] = dot_nn(hi, proj_hi) + dot_nn(lo, proj_hi) + dot_nn(hi, proj_lo)
        lax.fori_loop(i * (NB // 4), (i + 1) * (NB // 4), to_blocks, 0)
        push(*swap_part(i))

    def came(spot, send, recv):
        remote(spot, spot, send, recv, mate).wait_recv()

    ahead = []
    for o in range(1, NL):
        to = turn(zl, o, NL)
        ahead.append((to, remote(total_z.at[to], part_z.at[o - 1], rz_send.at[o - 1], rz_recv.at[o - 1], at(zl_=to))))
        sends.append(ahead[-1][1])
    for i in range(2):
        remote(*swap_part(i)).wait_recv()

        def add_swap(b, carry):
            value = halves[core, b] + swap[b]
            total_y[lax.div(b, NY), lax.rem(b, NY)] = value[:CUT]
            total_z[lax.div(b, NY), lax.rem(b, NY)] = value[CUT:]
            return carry

        lax.fori_loop(i * (NB // 2), (i + 1) * (NB // 2), add_swap, 0)
        for to, copy in ahead:
            pl.when(lax.div(to, NL // 2) == i)(copy.start)
        part = pl.ds(i * (NL // 2), NL // 2)
        for o in range(1, NY):
            to = turn(y, o, NY)
            push(total_y.at[part, to], part_y.at[o - 1, part], ry_send.at[i, o - 1], ry_recv.at[i, o - 1], at(y_=to))

    for i in range(2):
        part = pl.ds(i * (NL // 2), NL // 2)
        value = total_y[part, y]
        for o in range(1, NY):
            came(part_y.at[o - 1, part], ry_send.at[i, o - 1], ry_recv.at[i, o - 1])
            value += part_y[o - 1, part]
        mid_y[part] = value
    for o in range(1, NL):
        to = turn(zl, o, NL)
        push(mid_y.at[to], last_y.at[o - 1], tz_send.at[o - 1], tz_recv.at[o - 1], at(zl_=to))
    value = total_z[zl]
    for o in range(1, NL):
        came(part_z.at[o - 1], rz_send.at[o - 1], rz_recv.at[o - 1])
        value += part_z[o - 1]
    mid_z[...] = value
    for o in range(1, NY):
        to = turn(y, o, NY)
        push(mid_z.at[to], last_z.at[o - 1], ty_send.at[o - 1], ty_recv.at[o - 1], at(y_=to))

    def adam(g, rows):
        first_new = beta_first * fmb[rows] + (1.0 - beta_first) * g
        second_new = beta_second * smb[rows] + (1.0 - beta_second) * g * g
        fn_b[rows] = first_new
        sn_b[rows] = second_new
        return first_new / (jnp.sqrt(second_new) + adam_epsilon)

    own_y, rest_y = dirs_y.at[core, 0, y], dirs_y.at[core, pl.ds(1, NL - 1), y]
    own_z, rest_z = dirs_z.at[core, zl, 0], dirs_z.at[core, zl, pl.ds(1, NY - 1)]

    value = mid_y[zl]
    for o in range(1, NL):
        came(last_y.at[o - 1], tz_send.at[o - 1], tz_recv.at[o - 1])
        value += last_y[o - 1]
    dirs_y[core, 0, y] = adam(value, pl.ds(0, CUT))
    for o in range(1, NL):
        push(own_y, dirs_y.at[core, o, y], gz_send.at[o - 1], gz_recv.at[o - 1], at(zl_=turn(zl, o, NL)))
    for o in range(1, NY):
        push(own_y, own_y, ga_send.at[o - 1], ga_recv.at[o - 1], at(y_=turn(y, o, NY)))
    value = mid_z[y]
    for o in range(1, NY):
        came(last_z.at[o - 1], ty_send.at[o - 1], ty_recv.at[o - 1])
        value += last_z[o - 1]
    dirs_z[core, zl, 0] = adam(value, pl.ds(CUT, BLOCK - CUT))
    for o in range(1, NY):
        push(own_z, dirs_z.at[core, zl, o], gy_send.at[o - 1], gy_recv.at[o - 1], at(y_=turn(y, o, NY)))
    for o in range(1, NL):
        push(own_z, own_z, gb_send.at[o - 1], gb_recv.at[o - 1], at(zl_=turn(zl, o, NL)))
    for i, (src, dst) in enumerate(((fn_b, fn_x), (sn_b, sn_x))):
        remote(src, dst, o_send.at[i], o_recv.at[i], mate).start()
    for o in range(1, NL):
        came(dirs_y.at[core, o, y], gz_send.at[o - 1], gz_recv.at[o - 1])
    for o in range(1, NY):
        push(rest_y, rest_y, gc_send.at[o - 1], gc_recv.at[o - 1], at(y_=turn(y, o, NY)))
    for o in range(1, NY):
        came(dirs_z.at[core, zl, o], gy_send.at[o - 1], gy_recv.at[o - 1])
    for o in range(1, NL):
        push(rest_z, rest_z, gd_send.at[o - 1], gd_recv.at[o - 1], at(zl_=turn(zl, o, NL)))
    spot = dirs_y.at[core, :, y]
    push(spot, spot, gm_send.at[0], gm_recv.at[0], mate)
    spot = dirs_z.at[core, zl]
    push(spot, spot, gm_send.at[NY], gm_recv.at[NY], mate)

    loads[6].wait()

    for i, (own, other, out) in enumerate(((fn_b, fn_x, fn_out), (sn_b, sn_x, sn_out))):
        copy = remote(own, other, o_send.at[i], o_recv.at[i], mate)
        copy.wait_recv()
        for g in range(2):
            base = g * 2 * SHARE
            mine = jnp.where(first, own[pl.ds(base, SHARE), :], own[pl.ds(base + SHARE, SHARE), :])
            theirs = jnp.where(first, other[pl.ds(base, SHARE), :], other[pl.ds(base + SHARE, SHARE), :])
            out[:, g, pl.ds(0, HALF)] = jnp.where(first, mine, theirs)
            out[:, g, pl.ds(HALF, HALF)] = jnp.where(first, theirs, mine)
        copy.wait_send()

    for o in range(1, NY):
        source = turn(y, -o, NY)
        came(dirs_y.at[core, 0, source], ga_send.at[o - 1], ga_recv.at[o - 1])
        came(dirs_y.at[core, pl.ds(1, NL - 1), source], gc_send.at[o - 1], gc_recv.at[o - 1])
        spot = dirs_y.at[core, :, source]
        push(spot, spot, gm_send.at[o], gm_recv.at[o], mate)
    for o in range(1, NL):
        source = turn(zl, -o, NL)
        came(dirs_z.at[core, source, 0], gb_send.at[o - 1], gb_recv.at[o - 1])
        came(dirs_z.at[core, source, pl.ds(1, NY - 1)], gd_send.at[o - 1], gd_recv.at[o - 1])
        spot = dirs_z.at[core, source]
        push(spot, spot, gm_send.at[NY + o], gm_recv.at[NY + o], mate)
    for o in range(NY):
        came(dirs_y.at[1 - core, :, turn(y, -o, NY)], gm_send.at[o], gm_recv.at[o])
    for o in range(NL):
        came(dirs_z.at[1 - core, turn(zl, -o, NL)], gm_send.at[NY + o], gm_recv.at[NY + o])

    def from_blocks(m, carry):
        rows = pl.ds(pl.multiple_of(m * BLOCK, BLOCK), BLOCK)
        n = 2 * SHARE
        for h in range(2):
            lanes = pl.ds(h * HALF, HALF)
            z_, y_ = lax.div(m, NY // 2), 2 * lax.rem(m, NY // 2)
            back = lax.rem(zl - z_ + NL, NL)
            even, odd = (
                jnp.concatenate([dirs_y[h, back, v], dirs_z[h, z_, lax.rem(y - v + NY, NY)]], axis=0) for v in (y_, y_ + 1)
            )
            dirs_w[0, rows, lanes] = jnp.concatenate([even[:n], odd[:n]], axis=0)
            dirs_w[1, rows, lanes] = jnp.concatenate([even[n:], odd[n:]], axis=0)
        return carry

    lax.fori_loop(0, NB // 2, from_blocks, 0)

    basis_own = bas[0, y, core]
    for g in range(2):
        hi, lo = split(dirs_w[g])
        lifted = dot_nt(basis_own, hi) + dot_nt(basis_own, lo)
        mas_out[g] = mas[g] - step_size * lifted

    for copy in sends:
        copy.wait_send()


def leave(a, b, c, a_out, b_out, c_out, sem):
    copies = [pltpu.make_async_copy(src, dst, sem.at[i]) for i, (src, dst) in enumerate(((a, a_out), (b, b_out), (c, c_out)))]
    for copy in copies:
        copy.start()
    for copy in copies:
        copy.wait()


def on_device(tokens, cotangent, weights, basis, master, first_moment, second_moment):
    dma, vmem = pltpu.SemaphoreType.DMA, pltpu.VMEM
    share = (SHARE, 2, RANK)
    scratch = [
        vmem((GROUP, D), BF16), vmem((2 * HID, D), BF16), vmem((NL, NY, 2, 64, RANK), BF16), vmem((GROUP, HID), BF16),
        vmem((2, 64, HID), F32), vmem(share, F32), vmem(share, F32), vmem(share, F32), vmem(share, F32),
        vmem((BLOCK, HALF), F32), vmem((BLOCK, HALF), F32),
        vmem((HID, GROUP), F32), vmem((2 * HID, GROUP), F32), vmem((2, HID, RANK), F32),
        vmem((2, NB, BLOCK, HALF), F32), vmem((NB, BLOCK, HALF), F32),
        vmem((NL, NY, CUT, HALF), F32), vmem((NL, NY, BLOCK - CUT, HALF), F32),
        vmem((NY - 1, NL, CUT, HALF), F32), vmem((NL - 1, NY, BLOCK - CUT, HALF), F32),
        vmem((NL, CUT, HALF), F32), vmem((NY, BLOCK - CUT, HALF), F32),
        vmem((NL - 1, CUT, HALF), F32), vmem((NY - 1, BLOCK - CUT, HALF), F32),
        vmem((2, NL, NY, CUT, HALF), F32), vmem((2, NL, NY, BLOCK - CUT, HALF), F32), vmem((2, HID, RANK), F32),
        vmem((BLOCK, HALF), F32), vmem((BLOCK, HALF), F32), vmem((BLOCK, HALF), F32), vmem((BLOCK, HALF), F32),
        dma((7,)),
    ]
    for shape in (
        (2, CHUNKS), (NH, 2, CHUNKS), (NH, 2, CHUNKS), (2,), (NL - 1,), (2, 4), (2, 4), (NY,),
        (2,), (2,), (2, NY - 1), (NL - 1,), (NY - 1,), (NL - 1,),
        (NL - 1,), (NY - 1,), (NY - 1,), (NL - 1,), (NY - 1,), (NL - 1,), (NY + NL,), (2,),
    ):
        scratch += [dma if shape is None else dma(shape)] * 2
    any_space = pl.BlockSpec(memory_space=pl.ANY)
    in_vmem = pl.BlockSpec(memory_space=pltpu.VMEM)
    master_new, first_new, second_new = pl.pallas_call(
        kernel,
        out_shape=(
            jax.ShapeDtypeStruct((2, 64, HID), F32),
            jax.ShapeDtypeStruct(share, F32),
            jax.ShapeDtypeStruct(share, F32),
        ),
        in_specs=[any_space] * 7,
        out_specs=(in_vmem,) * 3,
        scratch_shapes=scratch,
        compiler_params=pltpu.CompilerParams(
            collective_id=0, has_side_effects=True, vmem_limit_bytes=63 * 1024 * 1024
        ),
        name="step",
    )(
        tokens, cotangent, weights.reshape(2 * HID, D), basis, jnp.swapaxes(master, 1, 2), first_moment, second_moment
    )
    results = (master_new, first_new, second_new)
    master_new, first_new, second_new = pl.pallas_call(
        leave,
        out_shape=tuple(jax.ShapeDtypeStruct(a.shape, a.dtype) for a in results),
        in_specs=[any_space] * 3,
        out_specs=(any_space,) * 3,
        scratch_shapes=[dma((3,))],
        name="leave",
    )(*results)
    return jnp.swapaxes(master_new, 1, 2), first_new, second_new


def solution(mesh):
    in_specs = (
        P(("dp", "hid"), None),
        P("dp", "hid"),
        P(None, "hid", None),
        P("dp", None),
        P(None, "hid", "dp"),
        P(("hid", "dp"), None, None),
        P(("hid", "dp"), None, None),
    )
    out_specs = (P(None, "hid", "dp"), P(("hid", "dp"), None, None), P(("hid", "dp"), None, None))
    return jax.shard_map(
        on_device, mesh=mesh, in_specs=in_specs, out_specs=out_specs, check_vma=False
    )
```

```python
import functools

import jax
import jax.numpy as jnp
from jax import lax
from jax.experimental import pallas as pl
from jax.experimental.pallas import tpu as pltpu
from jax.sharding import PartitionSpec as P

MESH = pl.DeviceIdType.MESH
F32 = jnp.float32
BF16 = jnp.bfloat16

beta_first = 0.9
beta_second = 0.95
step_size = 0.05
adam_epsilon = 1e-08

NX, NY, NL, NH = 4, 8, 4, 3
D, HID, RANK, TOK = 4096, 640, 256, 16
GROUP = 192
CHUNKS = 4
CW = D // CHUNKS
HALF = RANK // 2
SHARE = 10
BLOCK = 4 * SHARE
NB = NY * NL


def dot_nt(a, b):
    return lax.dot_general(a, b, (((1,), (1,)), ((), ())), preferred_element_type=F32)


def dot_nn(a, b):
    return lax.dot_general(a, b, (((1,), (0,)), ((), ())), preferred_element_type=F32)


def split(a):
    hi = a.astype(BF16)
    return hi, (a - hi.astype(F32)).astype(BF16)


def kernel(
    tok_in, cot_in, w_in, bas_in, mas_in, fm_in, sm_in,
    mas_out, fn_out, sn_out,
    tok, w, bas, cot, mas, fm, sm, fmx, smx, fmb, smb,
    cot_t, pre, grad, halves, swap, total, part_a, part_b, mid_a, mid_b, last_a, last_b,
    dirs, dirs_w, fn_b, sn_b, fn_x, sn_x,
    local_sem, z_send, z_recv, x_send, x_recv, xx_send, xx_recv, xd_send, xd_recv,
    bz_send, bz_recv, ya_send, ya_recv, yb_send, yb_recv, bc_send, bc_recv,
    m_send, m_recv, s_send, s_recv, r1_send, r1_recv, r2_send, r2_recv,
    g1_send, g1_recv, ga_send, ga_recv, gb_send, gb_recv, gc_send, gc_recv, o_send, o_recv,
):
    dp, hid = lax.axis_index("dp"), lax.axis_index("hid")
    core = lax.rem(dp, 2)
    y = lax.rem(lax.div(dp, 2), NY)
    zl = lax.div(dp, 2 * NY)
    x = lax.rem(hid, NX)
    zh = lax.div(hid, NX)

    def at(core_=core, y_=y, zl_=zl, x_=x, zh_=zh):
        return {"dp": (zl_ * NY + y_) * 2 + core_, "hid": zh_ * NX + x_}

    def turn(v, by, n):
        return lax.rem(v + (by + n), n)

    x_up, x_down, x_far = turn(x, 1, NX), turn(x, -1, NX), turn(x, 2, NX)
    mate = at(core_=1 - core)

    peers = [at(x_=x_up), at(x_=x_down), at(x_=x_far), mate]
    peers += [at(zh_=turn(zh, o, NH)) for o in range(1, NH)]
    peers += [at(zl_=turn(zl, o, NL)) for o in range(1, NL)]
    peers += [at(y_=turn(y, o, NY)) for o in range(1, NY)]

    loads = [
        pltpu.make_async_copy(tok_in, tok.at[pl.ds(pl.multiple_of(hid * TOK, TOK), TOK)], local_sem.at[0]),
        pltpu.make_async_copy(bas_in, bas.at[0, y, core], local_sem.at[1]),
        pltpu.make_async_copy(fm_in, fm, local_sem.at[2]),
        pltpu.make_async_copy(sm_in, sm, local_sem.at[3]),
        pltpu.make_async_copy(cot_in, cot, local_sem.at[4]),
        pltpu.make_async_copy(w_in, w, local_sem.at[5]),
        pltpu.make_async_copy(mas_in, mas, local_sem.at[6]),
    ]
    for load in loads:
        load.start()

    barrier = pltpu.get_barrier_semaphore()
    for peer in peers:
        pl.semaphore_signal(barrier, inc=1, device_id=peer, device_id_type=MESH)
    pl.semaphore_wait(barrier, len(peers))

    sends = []

    def remote(src, dst, send, recv, to):
        return pltpu.make_async_remote_copy(
            src_ref=src, dst_ref=dst, send_sem=send, recv_sem=recv, device_id=to, device_id_type=MESH
        )

    def push(*args):
        copy = remote(*args)
        copy.start()
        sends.append(copy)

    def rows_of(zh_, x_):
        return pl.ds(pl.multiple_of((zh_ * NX + x_) * TOK, TOK), TOK)

    def columns(k, half=None):
        if half is None:
            return pl.ds(k * CW, CW)
        return pl.ds(k * CW + half * (CW // 2), CW // 2)

    own_rows = rows_of(zh, x)

    def send_z(k):
        for o in (1, 2):
            push(tok_in.at[:, columns(k)], tok.at[own_rows, columns(k)], z_send.at[o - 1, k], z_recv.at[o - 1, k],
                 at(zh_=turn(zh, o, NH)))

    def wait_z(k):
        for o in (1, 2):
            spot = tok.at[rows_of(turn(zh, -o, NH), x), columns(k)]
            remote(spot, spot, z_send.at[o - 1, k], z_recv.at[o - 1, k], at(zh_=turn(zh, -o, NH))).wait_recv()

    def send_x(h, k):
        rows = rows_of(turn(zh, -h, NH), x)
        src = tok_in.at[:, columns(k)] if h == 0 else tok.at[rows, columns(k)]
        for d, to in enumerate((x_up, x_down)):
            push(src, tok.at[rows, columns(k)], x_send.at[h, d, k], x_recv.at[h, d, k], at(x_=to))

    def pass_x(h, k):
        source = turn(zh, -h, NH)
        for d, (came, to) in enumerate(((x_down, x_up), (x_up, x_down))):
            spot = tok.at[rows_of(source, came), columns(k)]
            remote(spot, spot, x_send.at[h, d, k], x_recv.at[h, d, k], at(x_=came)).wait_recv()
            piece = tok.at[rows_of(source, came), columns(k, d)]
            push(piece, piece, xx_send.at[h, d, k], xx_recv.at[h, d, k], at(x_=to))

    def send_far(h):
        spot = tok.at[rows_of(turn(zh, -h, NH), x), columns(CHUNKS - 1)]
        push(spot, spot, xd_send.at[h - 1], xd_recv.at[h - 1], at(x_=x_far))

    def wait_x(h, k):
        for d, came in enumerate((x_down, x_up)):
            spot = tok.at[rows_of(turn(zh, -h, NH), came), columns(k)]
            remote(spot, spot, x_send.at[h, d, k], x_recv.at[h, d, k], at(x_=came)).wait_recv()

    def wait_xx(k):
        for h in range(NH):
            rows = rows_of(turn(zh, -h, NH), x_far)
            if h > 0 and k == CHUNKS - 1:
                spot = tok.at[rows, columns(k)]
                remote(spot, spot, xd_send.at[h - 1], xd_recv.at[h - 1], at(x_=x_far)).wait_recv()
                continue
            for d in range(2):
                piece = tok.at[rows, columns(k, d)]
                remote(piece, piece, xx_send.at[h, d, k], xx_recv.at[h, d, k], at(x_=x_up)).wait_recv()

    def shards(part, by, half=None, core_=core):
        spot = (0 if part == 0 else pl.ds(1, NL - 1), turn(y, by, NY), core_)
        return bas.at[spot if half is None else spot + (pl.ds(32 * half, 32),)]

    steps = (1, -1, 2, -2)
    later = ((-3, None), (-4, 0), (3, None), (4, 1))

    def send_bz():
        for o in range(1, NL):
            push(bas_in, bas.at[o, y, core], bz_send.at[o - 1], bz_recv.at[o - 1], at(zl_=turn(zl, o, NL)))

    def wait_bz():
        for o in range(1, NL):
            spot = bas.at[o, y, core]
            remote(spot, spot, bz_send.at[o - 1], bz_recv.at[o - 1], at(zl_=turn(zl, -o, NL))).wait_recv()

    def send_ya(part):
        for i, step in enumerate(steps):
            src = bas_in if part == 0 else shards(1, 0)
            push(src, shards(part, 0), ya_send.at[part, i], ya_recv.at[part, i], at(y_=turn(y, step, NY)))

    def pass_y(part):
        for i in (2, 3, 0, 1):
            spot = shards(part, -steps[i])
            remote(spot, spot, ya_send.at[part, i], ya_recv.at[part, i], at(y_=turn(y, -steps[i], NY))).wait_recv()
            if i >= 2:
                sign, d = (1, 0) if i == 2 else (-1, 1)
                push(spot, spot, yb_send.at[part, 2 * d], yb_recv.at[part, 2 * d], at(y_=turn(y, sign, NY)))
                piece = shards(part, -steps[i], d)
                push(piece, piece, yb_send.at[part, 2 * d + 1], yb_recv.at[part, 2 * d + 1], at(y_=turn(y, 2 * sign, NY)))

    def wait_yb(part):
        for i, (by, half) in enumerate(later):
            spot = shards(part, by, half)
            remote(spot, spot, yb_send.at[part, i], yb_recv.at[part, i], at(y_=turn(y, 1, NY))).wait_recv()

    def send_bc(by):
        spot = bas.at[:, turn(y, by, NY), core]
        push(spot, spot, bc_send.at[by % NY], bc_recv.at[by % NY], mate)

    def wait_bc():
        for by in range(NY):
            spot = bas.at[:, turn(y, by, NY), 1 - core]
            remote(spot, spot, bc_send.at[by], bc_recv.at[by], mate).wait_recv()

    def products(k):
        def body(i, carry):
            rows = pl.ds(pl.multiple_of(i * HID, HID), HID)
            term = dot_nt(w[rows, columns(k)], tok[:, columns(k)])
            if k == 0:
                pre[rows, :] = term
            else:
                pre[rows, :] += term
            return carry

        lax.fori_loop(0, 2, body, 0)

    def project(k):
        slab = bas[turn(zl, -k, NL)].reshape(CW, RANK)
        return dot_nn(tok[:, columns(k)], slab)

    send_bz()
    send_z(0)
    send_ya(0)
    for k in range(CHUNKS):
        send_x(0, k)
    send_z(1)
    push(fm_in, fmx, m_send.at[0], m_recv.at[0], mate)
    push(sm_in, smx, m_send.at[1], m_recv.at[1], mate)
    loads[1].wait()
    loads[4].wait()
    wait_bz()
    send_ya(1)
    send_bc(0)
    cot_t[...] = cot[...].astype(F32).T

    wait_z(0)
    send_z(2)
    send_x(1, 0)
    send_x(2, 0)
    pass_x(0, 0)
    pass_x(0, 1)
    pass_y(0)
    wait_z(1)
    send_z(3)
    send_x(1, 1)
    send_x(2, 1)
    pass_x(0, 2)
    pass_x(0, 3)
    pass_x(1, 0)
    pass_x(2, 0)
    wait_z(2)
    send_x(1, 2)
    send_x(2, 2)
    pass_y(1)
    for by in (1, -1, 2, -2):
        send_bc(by)
    pass_x(1, 1)
    pass_x(2, 1)
    wait_z(3)
    send_x(1, 3)
    send_x(2, 3)
    send_far(1)
    send_far(2)
    pass_x(1, 2)
    pass_x(2, 2)
    loads[0].wait()
    loads[5].wait()
    wait_xx(0)
    products(0)
    wait_xx(1)
    products(1)
    wait_yb(0)
    wait_yb(1)
    for by in (3, -3, 4):
        send_bc(by)

    loads[2].wait()
    loads[3].wait()
    for i, spot in enumerate((fmx, smx)):
        remote(spot, spot, m_send.at[i], m_recv.at[i], mate).wait_recv()
    first = core == 0
    for own, other, block in ((fm, fmx, fmb), (sm, smx, smb)):
        for g in range(2):
            mine, theirs = own[:, g, :], other[:, g, :]
            low = jnp.where(first, mine, theirs)
            high = jnp.where(first, theirs, mine)
            base = g * 2 * SHARE
            block[pl.ds(base, SHARE), :] = jnp.where(first, low[:, :HALF], low[:, HALF:])
            block[pl.ds(base + SHARE, SHARE), :] = jnp.where(first, high[:, :HALF], high[:, HALF:])

    wait_xx(2)
    products(2)
    wait_bc()
    projected = project(0)
    for k in range(1, CHUNKS - 1):
        projected += project(k)
    wait_x(1, 3)
    wait_x(2, 3)
    wait_xx(3)
    products(3)

    proj_hi, proj_lo = split(projected + project(CHUNKS - 1))

    PART = HID // 2

    def to_blocks(m, carry):
        rows = pl.ds(pl.multiple_of(m * BLOCK, BLOCK), BLOCK)
        gate, up = grad[0, rows, :], grad[1, rows, :]
        n = 2 * SHARE
        for j in range(2):
            for h in range(2):
                lanes = slice(h * HALF, (h + 1) * HALF)
                halves[h, 2 * m + j, pl.ds(0, n), :] = gate[j * n:(j + 1) * n, lanes]
                halves[h, 2 * m + j, pl.ds(n, n), :] = up[j * n:(j + 1) * n, lanes]
        return carry

    def swap_part(i):
        part = pl.ds(i * (NB // 2), NB // 2)
        return halves.at[1 - core, part], swap.at[part], s_send.at[i], s_recv.at[i], mate

    for i in range(2):
        rows, up_rows = pl.ds(i * PART, PART), pl.ds(HID + i * PART, PART)
        pre_gate, pre_up, upstream = pre[rows, :], pre[up_rows, :], cot_t[rows, :]
        s = jax.nn.sigmoid(pre_gate)
        grad_gate = upstream * pre_up * (s * (1.0 + pre_gate * (1.0 - s)))
        grad_up = upstream * (pre_gate * s)
        for g, value in enumerate((grad_gate, grad_up)):
            hi, lo = split(value)
            grad[g, rows, :] = dot_nn(hi, proj_hi) + dot_nn(lo, proj_hi) + dot_nn(hi, proj_lo)
        lax.fori_loop(i * (NB // 4), (i + 1) * (NB // 4), to_blocks, 0)
        push(*swap_part(i))

    def add_part(i):
        remote(*swap_part(i)).wait_recv()

        def add_swap(b, carry):
            total[lax.div(b, NY), lax.rem(b, NY)] = halves[core, b] + swap[b]
            return carry

        lax.fori_loop(i * (NB // 2), (i + 1) * (NB // 2), add_swap, 0)

    def adam(g):
        first_new = beta_first * fmb[...] + (1.0 - beta_first) * g
        second_new = beta_second * smb[...] + (1.0 - beta_second) * g * g
        fn_b[...] = first_new
        sn_b[...] = second_new
        return first_new / (jnp.sqrt(second_new) + adam_epsilon)

    def swap_outputs():
        for i, (src, dst) in enumerate(((fn_b, fn_x), (sn_b, sn_x))):
            remote(src, dst, o_send.at[i], o_recv.at[i], mate).start()

    @pl.when(core == 0)
    def _():
        copies = []

        def go(*args):
            copy = remote(*args)
            copy.start()
            copies.append(copy)

        def came(spot, send, recv):
            remote(spot, spot, send, recv, mate).wait_recv()

        for i in range(2):
            add_part(i)
            part = pl.ds(i * (NL // 2), NL // 2)
            for o in range(1, NY):
                go(total.at[part, turn(y, o, NY)], part_a.at[o - 1, part], r1_send.at[i, o - 1], r1_recv.at[i, o - 1],
                   at(y_=turn(y, o, NY)))
        for i in range(2):
            part = pl.ds(i * (NL // 2), NL // 2)
            value = total[part, y]
            for o in range(1, NY):
                came(part_a.at[o - 1, part], r1_send.at[i, o - 1], r1_recv.at[i, o - 1])
                value += part_a[o - 1, part]
            mid_a[part] = value
        for o in range(1, NL):
            go(mid_a.at[turn(zl, o, NL)], last_a.at[o - 1], r2_send.at[o - 1], r2_recv.at[o - 1], at(zl_=turn(zl, o, NL)))
        value = mid_a[zl]
        for o in range(1, NL):
            came(last_a.at[o - 1], r2_send.at[o - 1], r2_recv.at[o - 1])
            value += last_a[o - 1]
        own, rest = dirs.at[0, 0, y], dirs.at[0, pl.ds(1, NL - 1), y]
        dirs[0, 0, y] = adam(value)
        for o in range(1, NL):
            go(own, dirs.at[0, o, y], g1_send.at[o - 1], g1_recv.at[o - 1], at(zl_=turn(zl, o, NL)))
        for o in range(1, NY):
            go(own, own, ga_send.at[o - 1], ga_recv.at[o - 1], at(y_=turn(y, o, NY)))
        swap_outputs()
        for o in range(1, NL):
            came(dirs.at[0, o, y], g1_send.at[o - 1], g1_recv.at[o - 1])
        for o in range(1, NY):
            go(rest, rest, gb_send.at[o - 1], gb_recv.at[o - 1], at(y_=turn(y, o, NY)))
        go(dirs.at[0, :, y], dirs.at[0, :, y], gc_send.at[0], gc_recv.at[0], mate)
        for o in range(1, NY):
            source = turn(y, -o, NY)
            came(dirs.at[0, 0, source], ga_send.at[o - 1], ga_recv.at[o - 1])
            came(dirs.at[0, pl.ds(1, NL - 1), source], gb_send.at[o - 1], gb_recv.at[o - 1])
            go(dirs.at[0, :, source], dirs.at[0, :, source], gc_send.at[o], gc_recv.at[o], mate)
        for o in range(NL):
            came(dirs.at[1, turn(zl, -o, NL)], gc_send.at[NY + o], gc_recv.at[NY + o])
        for copy in copies:
            copy.wait_send()

    @pl.when(core == 1)
    def _():
        copies = []

        def go(*args):
            copy = remote(*args)
            copy.start()
            copies.append(copy)

        def came(spot, send, recv):
            remote(spot, spot, send, recv, mate).wait_recv()

        firsts = []
        for o in range(1, NL):
            to = turn(zl, o, NL)
            firsts.append((to, remote(total.at[to], part_b.at[o - 1], r1_send.at[0, o - 1], r1_recv.at[0, o - 1], at(zl_=to))))
        for i in range(2):
            add_part(i)
            for to, copy in firsts:
                pl.when(lax.div(to, NL // 2) == i)(copy.start)
        value = total[zl]
        for o in range(1, NL):
            came(part_b.at[o - 1], r1_send.at[0, o - 1], r1_recv.at[0, o - 1])
            value += part_b[o - 1]
        mid_b[...] = value
        for o in range(1, NY):
            go(mid_b.at[turn(y, o, NY)], last_b.at[o - 1], r2_send.at[o - 1], r2_recv.at[o - 1], at(y_=turn(y, o, NY)))
        value = mid_b[y]
        for o in range(1, NY):
            came(last_b.at[o - 1], r2_send.at[o - 1], r2_recv.at[o - 1])
            value += last_b[o - 1]
        own, rest = dirs.at[1, zl, 0], dirs.at[1, zl, pl.ds(1, NY - 1)]
        dirs[1, zl, 0] = adam(value)
        for o in range(1, NY):
            go(own, dirs.at[1, zl, o], g1_send.at[o - 1], g1_recv.at[o - 1], at(y_=turn(y, o, NY)))
        for o in range(1, NL):
            go(own, own, ga_send.at[o - 1], ga_recv.at[o - 1], at(zl_=turn(zl, o, NL)))
        swap_outputs()
        for o in range(1, NY):
            came(dirs.at[1, zl, o], g1_send.at[o - 1], g1_recv.at[o - 1])
        for o in range(1, NL):
            go(rest, rest, gb_send.at[o - 1], gb_recv.at[o - 1], at(zl_=turn(zl, o, NL)))
        go(dirs.at[1, zl], dirs.at[1, zl], gc_send.at[NY], gc_recv.at[NY], mate)
        for o in range(1, NL):
            source = turn(zl, -o, NL)
            came(dirs.at[1, source, 0], ga_send.at[o - 1], ga_recv.at[o - 1])
            came(dirs.at[1, source, pl.ds(1, NY - 1)], gb_send.at[o - 1], gb_recv.at[o - 1])
            go(dirs.at[1, source], dirs.at[1, source], gc_send.at[NY + o], gc_recv.at[NY + o], mate)
        for o in range(NY):
            source = turn(y, -o, NY)
            came(dirs.at[0, :, source], gc_send.at[o], gc_recv.at[o])
        for to, copy in firsts:
            copy.wait_send()
        for copy in copies:
            copy.wait_send()

    for i, (own, other, out) in enumerate(((fn_b, fn_x, fm), (sn_b, sn_x, sm))):
        copy = remote(own, other, o_send.at[i], o_recv.at[i], mate)
        copy.wait_recv()
        for g in range(2):
            base = g * 2 * SHARE
            mine = jnp.where(first, own[pl.ds(base, SHARE), :], own[pl.ds(base + SHARE, SHARE), :])
            theirs = jnp.where(first, other[pl.ds(base, SHARE), :], other[pl.ds(base + SHARE, SHARE), :])
            out[:, g, pl.ds(0, HALF)] = jnp.where(first, mine, theirs)
            out[:, g, pl.ds(HALF, HALF)] = jnp.where(first, theirs, mine)
        copy.wait_send()
    leaving = [
        pltpu.make_async_copy(fm, fn_out, local_sem.at[2]),
        pltpu.make_async_copy(sm, sn_out, local_sem.at[3]),
    ]
    for copy in leaving:
        copy.start()

    def from_blocks(m, carry):
        rows = pl.ds(pl.multiple_of(m * BLOCK, BLOCK), BLOCK)
        n = 2 * SHARE
        for h in range(2):
            lanes = pl.ds(h * HALF, HALF)
            z_, y_ = lax.div(m, NY // 2), 2 * lax.rem(m, NY // 2)
            if h == 0:
                back = lax.rem(zl - z_ + NL, NL)
                even, odd = dirs[0, back, y_], dirs[0, back, y_ + 1]
            else:
                even = dirs[1, z_, lax.rem(y - y_ + NY, NY)]
                odd = dirs[1, z_, lax.rem(y - y_ - 1 + NY, NY)]
            dirs_w[0, rows, lanes] = jnp.concatenate([even[:n], odd[:n]], axis=0)
            dirs_w[1, rows, lanes] = jnp.concatenate([even[n:], odd[n:]], axis=0)
        return carry

    lax.fori_loop(0, NB // 2, from_blocks, 0)

    loads[6].wait()
    basis_own = bas[0, y, core]
    for g in range(2):
        hi, lo = split(dirs_w[g])
        lifted = dot_nt(basis_own, hi) + dot_nt(basis_own, lo)
        mas[g] = mas[g] - step_size * lifted
        leaving.append(pltpu.make_async_copy(mas.at[g], mas_out.at[g], local_sem.at[4 + g]))
        leaving[-1].start()
    for copy in leaving:
        copy.wait()

    for copy in sends:
        copy.wait_send()


def leave(master, first, second, master_out, first_out, second_out, held, held_first, held_second, sem):
    trips = [(master.at[i], held.at[i], master_out.at[i]) for i in range(2)]
    trips += [(first, held_first, first_out), (second, held_second, second_out)]
    ins = [pltpu.make_async_copy(src, spot, sem.at[0, i]) for i, (src, spot, _) in enumerate(trips)]
    outs = [pltpu.make_async_copy(spot, dst, sem.at[1, i]) for i, (_, spot, dst) in enumerate(trips)]
    for copy in ins:
        copy.start()
    for came, copy in zip(ins, outs):
        came.wait()
        copy.start()
    for copy in outs:
        copy.wait()


def on_device(tokens, cotangent, weights, basis, master, first_moment, second_moment):
    dma, vmem = pltpu.SemaphoreType.DMA, pltpu.VMEM
    share = (SHARE, 2, RANK)
    scratch = [
        vmem((GROUP, D), BF16), vmem((2 * HID, D), BF16), vmem((NL, NY, 2, 64, RANK), BF16), vmem((GROUP, HID), BF16),
        vmem((2, 64, HID), F32), vmem(share, F32), vmem(share, F32), vmem(share, F32), vmem(share, F32),
        vmem((BLOCK, HALF), F32), vmem((BLOCK, HALF), F32),
        vmem((HID, GROUP), F32), vmem((2 * HID, GROUP), F32), vmem((2, HID, RANK), F32),
        vmem((2, NB, BLOCK, HALF), F32), vmem((NB, BLOCK, HALF), F32), vmem((NL, NY, BLOCK, HALF), F32),
        vmem((NY - 1, NL, BLOCK, HALF), F32), vmem((NL - 1, NY, BLOCK, HALF), F32),
        vmem((NL, BLOCK, HALF), F32), vmem((NY, BLOCK, HALF), F32),
        vmem((NL - 1, BLOCK, HALF), F32), vmem((NY - 1, BLOCK, HALF), F32),
        vmem((2, NL, NY, BLOCK, HALF), F32), vmem((2, HID, RANK), F32),
        vmem((BLOCK, HALF), F32), vmem((BLOCK, HALF), F32), vmem((BLOCK, HALF), F32), vmem((BLOCK, HALF), F32),
        dma((7,)),
    ]
    for shape in (
        (2, CHUNKS), (NH, 2, CHUNKS), (NH, 2, CHUNKS), (2,), (NL - 1,), (2, 4), (2, 4), (NY,),
        (2,), (2,), (2, NY - 1), (NY - 1,), (NY - 1,), (NY - 1,), (NY - 1,), (NY + NL,), (2,),
    ):
        scratch += [dma if shape is None else dma(shape)] * 2
    any_space = pl.BlockSpec(memory_space=pl.ANY)
    master_new, first_new, second_new = pl.pallas_call(
        kernel,
        out_shape=(
            jax.ShapeDtypeStruct((2, 64, HID), F32),
            jax.ShapeDtypeStruct(share, F32),
            jax.ShapeDtypeStruct(share, F32),
        ),
        in_specs=[any_space] * 7,
        out_specs=(any_space,) * 3,
        scratch_shapes=scratch,
        compiler_params=pltpu.CompilerParams(
            collective_id=0, has_side_effects=True, vmem_limit_bytes=63 * 1024 * 1024
        ),
        name="step",
    )(
        tokens, cotangent, weights.reshape(2 * HID, D), basis, jnp.swapaxes(master, 1, 2), first_moment, second_moment
    )
    results = (master_new, first_new, second_new)
    master_new, first_new, second_new = pl.pallas_call(
        leave,
        out_shape=tuple(jax.ShapeDtypeStruct(a.shape, a.dtype) for a in results),
        in_specs=[any_space] * 3,
        out_specs=(any_space,) * 3,
        scratch_shapes=[vmem(a.shape, F32) for a in results] + [dma((2, 4))],
        name="leave",
    )(*results)
    return jnp.swapaxes(master_new, 1, 2), first_new, second_new


def solution(mesh):
    in_specs = (
        P(("dp", "hid"), None),
        P("dp", "hid"),
        P(None, "hid", None),
        P("dp", None),
        P(None, "hid", "dp"),
        P(("hid", "dp"), None, None),
        P(("hid", "dp"), None, None),
    )
    out_specs = (P(None, "hid", "dp"), P(("hid", "dp"), None, None), P(("hid", "dp"), None, None))
    return jax.shard_map(
        on_device, mesh=mesh, in_specs=in_specs, out_specs=out_specs, check_vma=False
    )
```

```python
import functools

import jax
import jax.numpy as jnp
from jax import lax
from jax.experimental import pallas as pl
from jax.experimental.pallas import tpu as pltpu
from jax.sharding import PartitionSpec as P

MESH = pl.DeviceIdType.MESH
F32 = jnp.float32
BF16 = jnp.bfloat16

beta_first = 0.9
beta_second = 0.95
step_size = 0.05
adam_epsilon = 1e-08

NX, NY, NL, NH = 4, 8, 4, 3
D, HID, RANK, TOK = 4096, 640, 256, 16
GROUP = 192
CHUNKS = 4
CW = D // CHUNKS
HALF = RANK // 2
SHARE = 10
BLOCK = 4 * SHARE
NB = NY * NL
AROUND = (4, 3, 5, 2, 6, 1, 7)


def dot_nt(a, b):
    return lax.dot_general(a, b, (((1,), (1,)), ((), ())), preferred_element_type=F32)


def dot_nn(a, b):
    return lax.dot_general(a, b, (((1,), (0,)), ((), ())), preferred_element_type=F32)


def split(a):
    hi = a.astype(BF16)
    return hi, (a - hi.astype(F32)).astype(BF16)


def kernel(
    tok_in, cot_in, w_in, bas_in, mas_in, fm_in, sm_in,
    mas_out, fn_out, sn_out,
    tok, w, bas, cot, mas, fm, sm, fmx, smx, fmb, smb,
    cot_t, pre, grad, halves, swap, total, part_a, part_b, mid_a, mid_b, last_a, last_b,
    dirs, dirs_w, fn_b, sn_b, fn_x, sn_x,
    local_sem, z_send, z_recv, x_send, x_recv, xx_send, xx_recv, xd_send, xd_recv,
    bz_send, bz_recv, ya_send, ya_recv, yb_send, yb_recv, bc_send, bc_recv,
    m_send, m_recv, s_send, s_recv, r1_send, r1_recv, r2_send, r2_recv,
    g1_send, g1_recv, ga_send, ga_recv, gb_send, gb_recv, gc_send, gc_recv, o_send, o_recv,
):
    dp, hid = lax.axis_index("dp"), lax.axis_index("hid")
    core = lax.rem(dp, 2)
    y = lax.rem(lax.div(dp, 2), NY)
    zl = lax.div(dp, 2 * NY)
    x = lax.rem(hid, NX)
    zh = lax.div(hid, NX)

    def at(core_=core, y_=y, zl_=zl, x_=x, zh_=zh):
        return {"dp": (zl_ * NY + y_) * 2 + core_, "hid": zh_ * NX + x_}

    def turn(v, by, n):
        return lax.rem(v + (by + n), n)

    x_up, x_down, x_far = turn(x, 1, NX), turn(x, -1, NX), turn(x, 2, NX)
    mate = at(core_=1 - core)

    peers = [at(x_=x_up), at(x_=x_down), at(x_=x_far), mate]
    peers += [at(zh_=turn(zh, o, NH)) for o in range(1, NH)]
    peers += [at(zl_=turn(zl, o, NL)) for o in range(1, NL)]
    peers += [at(y_=turn(y, o, NY)) for o in range(1, NY)]

    loads = [
        pltpu.make_async_copy(tok_in, tok.at[pl.ds(pl.multiple_of(hid * TOK, TOK), TOK)], local_sem.at[0]),
        pltpu.make_async_copy(bas_in, bas.at[0, y, core], local_sem.at[1]),
        pltpu.make_async_copy(fm_in, fm, local_sem.at[2]),
        pltpu.make_async_copy(sm_in, sm, local_sem.at[3]),
        pltpu.make_async_copy(cot_in, cot, local_sem.at[4]),
        pltpu.make_async_copy(w_in, w, local_sem.at[5]),
        pltpu.make_async_copy(mas_in, mas, local_sem.at[6]),
    ]
    barrier = pltpu.get_barrier_semaphore()
    for peer in peers:
        pl.semaphore_signal(barrier, inc=1, device_id=peer, device_id_type=MESH)
    for load in loads:
        load.start()
    pl.semaphore_wait(barrier, len(peers))

    sends = []

    def remote(src, dst, send, recv, to):
        return pltpu.make_async_remote_copy(
            src_ref=src, dst_ref=dst, send_sem=send, recv_sem=recv, device_id=to, device_id_type=MESH
        )

    def push(*args):
        copy = remote(*args)
        copy.start()
        sends.append(copy)

    def rows_of(zh_, x_):
        return pl.ds(pl.multiple_of((zh_ * NX + x_) * TOK, TOK), TOK)

    def columns(k, half=None):
        if half is None:
            return pl.ds(k * CW, CW)
        return pl.ds(k * CW + half * (CW // 2), CW // 2)

    own_rows = rows_of(zh, x)

    def send_z(k):
        for o in (1, 2):
            push(tok_in.at[:, columns(k)], tok.at[own_rows, columns(k)], z_send.at[o - 1, k], z_recv.at[o - 1, k],
                 at(zh_=turn(zh, o, NH)))

    def wait_z(k):
        for o in (1, 2):
            spot = tok.at[rows_of(turn(zh, -o, NH), x), columns(k)]
            remote(spot, spot, z_send.at[o - 1, k], z_recv.at[o - 1, k], at(zh_=turn(zh, -o, NH))).wait_recv()

    def send_x(h, k):
        rows = rows_of(turn(zh, -h, NH), x)
        src = tok_in.at[:, columns(k)] if h == 0 else tok.at[rows, columns(k)]
        for d, to in enumerate((x_up, x_down)):
            push(src, tok.at[rows, columns(k)], x_send.at[h, d, k], x_recv.at[h, d, k], at(x_=to))

    def pass_x(h, k):
        source = turn(zh, -h, NH)
        for d, (came, to) in enumerate(((x_down, x_up), (x_up, x_down))):
            spot = tok.at[rows_of(source, came), columns(k)]
            remote(spot, spot, x_send.at[h, d, k], x_recv.at[h, d, k], at(x_=came)).wait_recv()
            piece = tok.at[rows_of(source, came), columns(k, d)]
            push(piece, piece, xx_send.at[h, d, k], xx_recv.at[h, d, k], at(x_=to))

    def send_far(h):
        spot = tok.at[rows_of(turn(zh, -h, NH), x), columns(CHUNKS - 1)]
        push(spot, spot, xd_send.at[h - 1], xd_recv.at[h - 1], at(x_=x_far))

    def wait_x(h, k):
        for d, came in enumerate((x_down, x_up)):
            spot = tok.at[rows_of(turn(zh, -h, NH), came), columns(k)]
            remote(spot, spot, x_send.at[h, d, k], x_recv.at[h, d, k], at(x_=came)).wait_recv()

    def wait_xx(k):
        for h in range(NH):
            rows = rows_of(turn(zh, -h, NH), x_far)
            if h > 0 and k == CHUNKS - 1:
                spot = tok.at[rows, columns(k)]
                remote(spot, spot, xd_send.at[h - 1], xd_recv.at[h - 1], at(x_=x_far)).wait_recv()
                continue
            for d in range(2):
                piece = tok.at[rows, columns(k, d)]
                remote(piece, piece, xx_send.at[h, d, k], xx_recv.at[h, d, k], at(x_=x_up)).wait_recv()

    def shards(part, by, half=None, core_=core):
        spot = (0 if part == 0 else pl.ds(1, NL - 1), turn(y, by, NY), core_)
        return bas.at[spot if half is None else spot + (pl.ds(32 * half, 32),)]

    steps = (1, -1, 2, -2)
    later = ((-3, None), (-4, 0), (3, None), (4, 1))

    def send_bz():
        for o in range(1, NL):
            push(bas_in, bas.at[o, y, core], bz_send.at[o - 1], bz_recv.at[o - 1], at(zl_=turn(zl, o, NL)))

    def wait_bz():
        for o in range(1, NL):
            spot = bas.at[o, y, core]
            remote(spot, spot, bz_send.at[o - 1], bz_recv.at[o - 1], at(zl_=turn(zl, -o, NL))).wait_recv()

    def send_ya(part):
        for i, step in enumerate(steps):
            src = bas_in if part == 0 else shards(1, 0)
            push(src, shards(part, 0), ya_send.at[part, i], ya_recv.at[part, i], at(y_=turn(y, step, NY)))

    def pass_y(part):
        for i in (2, 3, 0, 1):
            spot = shards(part, -steps[i])
            remote(spot, spot, ya_send.at[part, i], ya_recv.at[part, i], at(y_=turn(y, -steps[i], NY))).wait_recv()
            if i >= 2:
                sign, d = (1, 0) if i == 2 else (-1, 1)
                push(spot, spot, yb_send.at[part, 2 * d], yb_recv.at[part, 2 * d], at(y_=turn(y, sign, NY)))
                piece = shards(part, -steps[i], d)
                push(piece, piece, yb_send.at[part, 2 * d + 1], yb_recv.at[part, 2 * d + 1], at(y_=turn(y, 2 * sign, NY)))

    def wait_yb(part):
        for i, (by, half) in enumerate(later):
            spot = shards(part, by, half)
            remote(spot, spot, yb_send.at[part, i], yb_recv.at[part, i], at(y_=turn(y, 1, NY))).wait_recv()

    def send_bc(by):
        spot = bas.at[:, turn(y, by, NY), core]
        push(spot, spot, bc_send.at[by % NY], bc_recv.at[by % NY], mate)

    def wait_bc():
        for by in range(NY):
            spot = bas.at[:, turn(y, by, NY), 1 - core]
            remote(spot, spot, bc_send.at[by], bc_recv.at[by], mate).wait_recv()

    def products(k):
        def body(i, carry):
            rows = pl.ds(pl.multiple_of(i * HID, HID), HID)
            term = dot_nt(w[rows, columns(k)], tok[:, columns(k)])
            if k == 0:
                pre[rows, :] = term
            else:
                pre[rows, :] += term
            return carry

        lax.fori_loop(0, 2, body, 0)

    def project(k):
        slab = bas[turn(zl, -k, NL)].reshape(CW, RANK)
        return dot_nn(tok[:, columns(k)], slab)

    send_z(0)
    send_bz()
    send_ya(0)
    for k in range(CHUNKS):
        send_x(0, k)
    send_z(1)
    push(fm_in, fmx, m_send.at[0], m_recv.at[0], mate)
    push(sm_in, smx, m_send.at[1], m_recv.at[1], mate)
    loads[1].wait()
    loads[4].wait()
    wait_bz()
    send_ya(1)
    send_bc(0)
    cot_t[...] = cot[...].astype(F32).T

    wait_z(0)
    send_z(2)
    send_x(1, 0)
    send_x(2, 0)
    pass_x(0, 0)
    pass_x(0, 1)
    pass_y(0)
    wait_z(1)
    send_z(3)
    send_x(1, 1)
    send_x(2, 1)
    pass_x(0, 2)
    pass_x(0, 3)
    pass_x(1, 0)
    pass_x(2, 0)
    wait_z(2)
    send_x(1, 2)
    send_x(2, 2)
    pass_y(1)
    for by in (1, -1, 2, -2):
        send_bc(by)
    pass_x(1, 1)
    pass_x(2, 1)
    wait_z(3)
    send_x(1, 3)
    send_x(2, 3)
    send_far(1)
    send_far(2)
    pass_x(1, 2)
    pass_x(2, 2)
    loads[0].wait()
    loads[5].wait()
    wait_xx(0)
    products(0)
    wait_xx(1)
    products(1)
    wait_yb(0)
    wait_yb(1)
    for by in (3, -3, 4):
        send_bc(by)

    loads[2].wait()
    loads[3].wait()
    for i, spot in enumerate((fmx, smx)):
        remote(spot, spot, m_send.at[i], m_recv.at[i], mate).wait_recv()
    first = core == 0
    for own, other, block in ((fm, fmx, fmb), (sm, smx, smb)):
        for g in range(2):
            mine, theirs = own[:, g, :], other[:, g, :]
            low = jnp.where(first, mine, theirs)
            high = jnp.where(first, theirs, mine)
            base = g * 2 * SHARE
            block[pl.ds(base, SHARE), :] = jnp.where(first, low[:, :HALF], low[:, HALF:])
            block[pl.ds(base + SHARE, SHARE), :] = jnp.where(first, high[:, :HALF], high[:, HALF:])

    wait_xx(2)
    products(2)
    wait_bc()
    projected = project(0)
    for k in range(1, CHUNKS - 1):
        projected += project(k)
    wait_x(1, 3)
    wait_x(2, 3)
    wait_xx(3)
    products(3)

    proj_hi, proj_lo = split(projected + project(CHUNKS - 1))

    PART = HID // 2

    def to_blocks(m, carry):
        rows = pl.ds(pl.multiple_of(m * BLOCK, BLOCK), BLOCK)
        gate, up = grad[0, rows, :], grad[1, rows, :]
        n = 2 * SHARE
        for j in range(2):
            for h in range(2):
                lanes = slice(h * HALF, (h + 1) * HALF)
                halves[h, 2 * m + j, pl.ds(0, n), :] = gate[j * n:(j + 1) * n, lanes]
                halves[h, 2 * m + j, pl.ds(n, n), :] = up[j * n:(j + 1) * n, lanes]
        return carry

    def swap_part(i):
        part = pl.ds(i * (NB // 2), NB // 2)
        return halves.at[1 - core, part], swap.at[part], s_send.at[i], s_recv.at[i], mate

    for i in range(2):
        rows, up_rows = pl.ds(i * PART, PART), pl.ds(HID + i * PART, PART)
        pre_gate, pre_up, upstream = pre[rows, :], pre[up_rows, :], cot_t[rows, :]
        s = jax.nn.sigmoid(pre_gate)
        grad_gate = upstream * pre_up * (s * (1.0 + pre_gate * (1.0 - s)))
        grad_up = upstream * (pre_gate * s)
        for g, value in enumerate((grad_gate, grad_up)):
            hi, lo = split(value)
            grad[g, rows, :] = dot_nn(hi, proj_hi) + dot_nn(lo, proj_hi) + dot_nn(hi, proj_lo)
        lax.fori_loop(i * (NB // 4), (i + 1) * (NB // 4), to_blocks, 0)
        push(*swap_part(i))

    def add_part(i):
        remote(*swap_part(i)).wait_recv()

        def add_swap(b, carry):
            total[lax.div(b, NY), lax.rem(b, NY)] = halves[core, b] + swap[b]
            return carry

        lax.fori_loop(i * (NB // 2), (i + 1) * (NB // 2), add_swap, 0)

    def adam(g):
        first_new = beta_first * fmb[...] + (1.0 - beta_first) * g
        second_new = beta_second * smb[...] + (1.0 - beta_second) * g * g
        fn_b[...] = first_new
        sn_b[...] = second_new
        return first_new / (jnp.sqrt(second_new) + adam_epsilon)

    def swap_outputs():
        for i, (src, dst) in enumerate(((fn_b, fn_x), (sn_b, sn_x))):
            remote(src, dst, o_send.at[i], o_recv.at[i], mate).start()

    @pl.when(core == 0)
    def _():
        copies = []

        def go(*args):
            copy = remote(*args)
            copy.start()
            copies.append(copy)

        def came(spot, send, recv):
            remote(spot, spot, send, recv, mate).wait_recv()

        for i in range(2):
            add_part(i)
            part = pl.ds(i * (NL // 2), NL // 2)
            for o in AROUND:
                go(total.at[part, turn(y, o, NY)], part_a.at[o - 1, part], r1_send.at[i, o - 1], r1_recv.at[i, o - 1],
                   at(y_=turn(y, o, NY)))
        for i in range(2):
            part = pl.ds(i * (NL // 2), NL // 2)
            value = total[part, y]
            for o in AROUND:
                came(part_a.at[o - 1, part], r1_send.at[i, o - 1], r1_recv.at[i, o - 1])
                value += part_a[o - 1, part]
            mid_a[part] = value
        for o in range(1, NL):
            go(mid_a.at[turn(zl, o, NL)], last_a.at[o - 1], r2_send.at[o - 1], r2_recv.at[o - 1], at(zl_=turn(zl, o, NL)))
        value = mid_a[zl]
        for o in range(1, NL):
            came(last_a.at[o - 1], r2_send.at[o - 1], r2_recv.at[o - 1])
            value += last_a[o - 1]
        own, rest = dirs.at[0, 0, y], dirs.at[0, pl.ds(1, NL - 1), y]
        dirs[0, 0, y] = adam(value)
        for o in range(1, NL):
            go(own, dirs.at[0, o, y], g1_send.at[o - 1], g1_recv.at[o - 1], at(zl_=turn(zl, o, NL)))
        for o in AROUND:
            go(own, own, ga_send.at[o - 1], ga_recv.at[o - 1], at(y_=turn(y, o, NY)))
        swap_outputs()
        for o in range(1, NL):
            came(dirs.at[0, o, y], g1_send.at[o - 1], g1_recv.at[o - 1])
        for o in AROUND:
            go(rest, rest, gb_send.at[o - 1], gb_recv.at[o - 1], at(y_=turn(y, o, NY)))
        go(dirs.at[0, :, y], dirs.at[0, :, y], gc_send.at[0], gc_recv.at[0], mate)
        for o in AROUND:
            source = turn(y, -o, NY)
            came(dirs.at[0, 0, source], ga_send.at[o - 1], ga_recv.at[o - 1])
            came(dirs.at[0, pl.ds(1, NL - 1), source], gb_send.at[o - 1], gb_recv.at[o - 1])
            go(dirs.at[0, :, source], dirs.at[0, :, source], gc_send.at[o], gc_recv.at[o], mate)
        near = zl + 1 - 2 * lax.rem(zl, 2)
        for n, source in enumerate((zl, turn(zl, 2, NL), near, turn(near, 2, NL))):
            came(dirs.at[1, source], gc_send.at[NY + n], gc_recv.at[NY + n])
        for copy in copies:
            copy.wait_send()

    @pl.when(core == 1)
    def _():
        copies = []

        def go(*args):
            copy = remote(*args)
            copy.start()
            copies.append(copy)

        def came(spot, send, recv):
            remote(spot, spot, send, recv, mate).wait_recv()

        firsts = []
        for o in range(1, NL):
            to = turn(zl, o, NL)
            firsts.append((to, remote(total.at[to], part_b.at[o - 1], r1_send.at[0, o - 1], r1_recv.at[0, o - 1], at(zl_=to))))
        for i in range(2):
            add_part(i)
            for to, copy in firsts:
                pl.when(lax.div(to, NL // 2) == i)(copy.start)
        value = total[zl]
        for o in range(1, NL):
            came(part_b.at[o - 1], r1_send.at[0, o - 1], r1_recv.at[0, o - 1])
            value += part_b[o - 1]
        mid_b[...] = value
        for o in AROUND:
            go(mid_b.at[turn(y, o, NY)], last_b.at[o - 1], r2_send.at[o - 1], r2_recv.at[o - 1], at(y_=turn(y, o, NY)))
        value = mid_b[y]
        for o in AROUND:
            came(last_b.at[o - 1], r2_send.at[o - 1], r2_recv.at[o - 1])
            value += last_b[o - 1]
        own = dirs.at[1, zl, 0]
        dirs[1, zl, 0] = adam(value)
        for o in AROUND:
            go(own, dirs.at[1, zl, o], g1_send.at[o - 1], g1_recv.at[o - 1], at(y_=turn(y, o, NY)))
        for o in range(1, NL):
            go(own, own, ga_send.at[o - 1], ga_recv.at[o - 1], at(zl_=turn(zl, o, NL)))
        swap_outputs()
        for o in AROUND:
            came(dirs.at[1, zl, o], g1_send.at[o - 1], g1_recv.at[o - 1])
        near = zl + 1 - 2 * lax.rem(zl, 2)
        far, last = turn(zl, 2, NL), turn(near, 2, NL)
        pieces = (pl.ds(1, 4), pl.ds(5, NY - 5))
        for i, piece in enumerate(pieces):
            spot = dirs.at[1, zl, piece]
            go(spot, spot, gb_send.at[i], gb_recv.at[i], at(zl_=far))
            go(spot, spot, gb_send.at[2 + i], gb_recv.at[2 + i], at(zl_=near))
        go(dirs.at[1, zl], dirs.at[1, zl], gc_send.at[NY], gc_recv.at[NY], mate)
        for i, piece in enumerate(pieces):
            spot = dirs.at[1, far, piece]
            came(spot, gb_send.at[i], gb_recv.at[i])
            go(spot, spot, gb_send.at[4 + i], gb_recv.at[4 + i], at(zl_=near))
        for o in range(1, NL):
            came(dirs.at[1, turn(zl, -o, NL), 0], ga_send.at[o - 1], ga_recv.at[o - 1])
        for n, source in enumerate((far, near, last)):
            if n > 0:
                for i, piece in enumerate(pieces):
                    came(dirs.at[1, source, piece], gb_send.at[2 * n + i], gb_recv.at[2 * n + i])
            go(dirs.at[1, source], dirs.at[1, source], gc_send.at[NY + 1 + n], gc_recv.at[NY + 1 + n], mate)
        for o in range(NY):
            source = turn(y, -o, NY)
            came(dirs.at[0, :, source], gc_send.at[o], gc_recv.at[o])
        for to, copy in firsts:
            copy.wait_send()
        for copy in copies:
            copy.wait_send()

    for i, (own, other, out) in enumerate(((fn_b, fn_x, fm), (sn_b, sn_x, sm))):
        copy = remote(own, other, o_send.at[i], o_recv.at[i], mate)
        copy.wait_recv()
        for g in range(2):
            base = g * 2 * SHARE
            mine = jnp.where(first, own[pl.ds(base, SHARE), :], own[pl.ds(base + SHARE, SHARE), :])
            theirs = jnp.where(first, other[pl.ds(base, SHARE), :], other[pl.ds(base + SHARE, SHARE), :])
            out[:, g, pl.ds(0, HALF)] = jnp.where(first, mine, theirs)
            out[:, g, pl.ds(HALF, HALF)] = jnp.where(first, theirs, mine)
        copy.wait_send()
    leaving = [
        pltpu.make_async_copy(fm, fn_out, local_sem.at[2]),
        pltpu.make_async_copy(sm, sn_out, local_sem.at[3]),
    ]
    for copy in leaving:
        copy.start()

    def from_blocks(m, carry):
        rows = pl.ds(pl.multiple_of(m * BLOCK, BLOCK), BLOCK)
        n = 2 * SHARE
        for h in range(2):
            lanes = pl.ds(h * HALF, HALF)
            z_, y_ = lax.div(m, NY // 2), 2 * lax.rem(m, NY // 2)
            if h == 0:
                back = lax.rem(zl - z_ + NL, NL)
                even, odd = dirs[0, back, y_], dirs[0, back, y_ + 1]
            else:
                even = dirs[1, z_, lax.rem(y - y_ + NY, NY)]
                odd = dirs[1, z_, lax.rem(y - y_ - 1 + NY, NY)]
            dirs_w[0, rows, lanes] = jnp.concatenate([even[:n], odd[:n]], axis=0)
            dirs_w[1, rows, lanes] = jnp.concatenate([even[n:], odd[n:]], axis=0)
        return carry

    lax.fori_loop(0, NB // 2, from_blocks, 0)

    loads[6].wait()
    basis_own = bas[0, y, core]
    for g in range(2):
        hi, lo = split(dirs_w[g])
        lifted = dot_nt(basis_own, hi) + dot_nt(basis_own, lo)
        mas[g] = mas[g] - step_size * lifted
        leaving.append(pltpu.make_async_copy(mas.at[g], mas_out.at[g], local_sem.at[4 + g]))
        leaving[-1].start()
    for copy in leaving:
        copy.wait()

    for copy in sends:
        copy.wait_send()


def leave(master, first, second, master_out, first_out, second_out, held, held_first, held_second, sem):
    trips = [(master.at[i], held.at[i], master_out.at[i]) for i in range(2)]
    trips += [(first, held_first, first_out), (second, held_second, second_out)]
    ins = [pltpu.make_async_copy(src, spot, sem.at[0, i]) for i, (src, spot, _) in enumerate(trips)]
    outs = [pltpu.make_async_copy(spot, dst, sem.at[1, i]) for i, (_, spot, dst) in enumerate(trips)]
    for copy in ins:
        copy.start()
    for came, copy in zip(ins, outs):
        came.wait()
        copy.start()
    for copy in outs:
        copy.wait()


def on_device(tokens, cotangent, weights, basis, master, first_moment, second_moment):
    dma, vmem = pltpu.SemaphoreType.DMA, pltpu.VMEM
    share = (SHARE, 2, RANK)
    scratch = [
        vmem((GROUP, D), BF16), vmem((2 * HID, D), BF16), vmem((NL, NY, 2, 64, RANK), BF16), vmem((GROUP, HID), BF16),
        vmem((2, 64, HID), F32), vmem(share, F32), vmem(share, F32), vmem(share, F32), vmem(share, F32),
        vmem((BLOCK, HALF), F32), vmem((BLOCK, HALF), F32),
        vmem((HID, GROUP), F32), vmem((2 * HID, GROUP), F32), vmem((2, HID, RANK), F32),
        vmem((2, NB, BLOCK, HALF), F32), vmem((NB, BLOCK, HALF), F32), vmem((NL, NY, BLOCK, HALF), F32),
        vmem((NY - 1, NL, BLOCK, HALF), F32), vmem((NL - 1, NY, BLOCK, HALF), F32),
        vmem((NL, BLOCK, HALF), F32), vmem((NY, BLOCK, HALF), F32),
        vmem((NL - 1, BLOCK, HALF), F32), vmem((NY - 1, BLOCK, HALF), F32),
        vmem((2, NL, NY, BLOCK, HALF), F32), vmem((2, HID, RANK), F32),
        vmem((BLOCK, HALF), F32), vmem((BLOCK, HALF), F32), vmem((BLOCK, HALF), F32), vmem((BLOCK, HALF), F32),
        dma((7,)),
    ]
    for shape in (
        (2, CHUNKS), (NH, 2, CHUNKS), (NH, 2, CHUNKS), (2,), (NL - 1,), (2, 4), (2, 4), (NY,),
        (2,), (2,), (2, NY - 1), (NY - 1,), (NY - 1,), (NY - 1,), (NY - 1,), (NY + NL,), (2,),
    ):
        scratch += [dma if shape is None else dma(shape)] * 2
    any_space = pl.BlockSpec(memory_space=pl.ANY)
    master_new, first_new, second_new = pl.pallas_call(
        kernel,
        out_shape=(
            jax.ShapeDtypeStruct((2, 64, HID), F32),
            jax.ShapeDtypeStruct(share, F32),
            jax.ShapeDtypeStruct(share, F32),
        ),
        in_specs=[any_space] * 7,
        out_specs=(any_space,) * 3,
        scratch_shapes=scratch,
        compiler_params=pltpu.CompilerParams(
            collective_id=0, has_side_effects=True, vmem_limit_bytes=63 * 1024 * 1024
        ),
        name="step",
    )(
        tokens, cotangent, weights.reshape(2 * HID, D), basis, jnp.swapaxes(master, 1, 2), first_moment, second_moment
    )
    results = (master_new, first_new, second_new)
    master_new, first_new, second_new = pl.pallas_call(
        leave,
        out_shape=tuple(jax.ShapeDtypeStruct(a.shape, a.dtype) for a in results),
        in_specs=[any_space] * 3,
        out_specs=(any_space,) * 3,
        scratch_shapes=[vmem(a.shape, F32) for a in results] + [dma((2, 4))],
        name="leave",
    )(*results)
    return jnp.swapaxes(master_new, 1, 2), first_new, second_new


def solution(mesh):
    in_specs = (
        P(("dp", "hid"), None),
        P("dp", "hid"),
        P(None, "hid", None),
        P("dp", None),
        P(None, "hid", "dp"),
        P(("hid", "dp"), None, None),
        P(("hid", "dp"), None, None),
    )
    out_specs = (P(None, "hid", "dp"), P(("hid", "dp"), None, None), P(("hid", "dp"), None, None))
    return jax.shard_map(
        on_device, mesh=mesh, in_specs=in_specs, out_specs=out_specs, check_vma=False
    )
```
